32 devices in a mesh: basis: 4 (over y, x), docs: 8 (over z, core).
Axes of the slice: x: 2, y: 2, z: 4, core: 2. Of those that a mesh axis runs over, the one named last changes fastest.
Arguments:
- eig_in: bfloat16 [28672, 28672], P('basis', 'docs'), may hold values from -0.03125 to 0.03125
- eig_out: bfloat16 [8192, 8192], P('basis', 'docs'), may hold values from -0.0625 to 0.0625
- eigvals: bfloat16 [8192, 28672], P('basis', 'docs'), may hold values from 0.0025 to 3.6
- out_factors: bfloat16 [8192, 256], P('docs'), may hold values from -1.1953125 to 1.1953125
- in_factors: bfloat16 [28672, 256], P(('basis', 'docs')), may hold values from -1.1953125 to 1.1953125
- test_matrix: bfloat16 [28672, 32], P('docs'), may hold values from -0.03125 to 0.03125
- activations: bfloat16 [1024, 28672], P('docs', 'basis'), may hold values from -6 to 6
- gradients: bfloat16 [1024, 8192], P('docs', 'basis'), may hold values from -0.00059890747 to 0.00059890747
- doc_lengths: int32 [32], replicated, may hold values from 1 to 96, 1024 in all
Outputs:
- scores: float32 [1024, 4], P('docs')
- doc_influence: float32 [32, 4], replicated
The draws below stay inside these ranges and needn't reach their ends.
Inputs may be any that keep to these rules, and one draw needn't show every extreme that they name: `doc_lengths`: the documents lie end to end in token order and their lengths sum to 1024.
All inputs are finite; a program needn't handle non-finite values.
Results may differ from the reference program's by a relative error of at most 0.0085.
Values may be sent and summed in bfloat16 or wider, within the bound.
No kernel may reach another device: no remote copies, remote signals or barrier semaphores. Data moves between devices by JAX's collectives and lax.ppermute only.
A program may use at most 320 MiB of HBM per device.

```python
import math
import jax
import jax.numpy as jnp
import numpy as np
from jax import lax

D = 8192
FF = 28672
QUERIES = 4
LQ = 64
RANK = 32
TOKENS = 1024
DOCUMENTS = 32
DOC_MOST = 96
QCOLS = 256


def draw_eigvals(key, part):
    row_place = jnp.arange(D, dtype=jnp.float32)[:, None] / D
    col_place = jnp.arange(FF, dtype=jnp.float32)[None, :] / FF
    rough_part = jax.random.uniform(key, (D, FF), jnp.float32, 0.3, 1.7)
    profile = jnp.exp(-3.0 * row_place - 2.0 * col_place)
    return (2.0 * profile * rough_part).astype(jnp.bfloat16)


def block_levels(key, extent, shards, smallest, high):
    def one(dim, parts):
        steps = jax.random.uniform(jax.random.fold_in(jax.random.fold_in(key, 6), dim), (parts,), jnp.float32, smallest / len(shards), high / len(shards))
        return jnp.repeat(jnp.exp(steps), extent[dim] // parts).reshape((-1,) + (1,) * (len(extent) - dim - 1))

    level = one(*shards[0])
    for cut in shards[1:]:
        level = level * one(*cut)
    return level


def split_up(number_of, total, limit, lean):
    portions = [(1 << 20) // math.isqrt(standing ** lean) + 1 for standing in range(2, number_of + 1)]
    surplus, counts = total - limit - (number_of - 1), [1] * (number_of - 1)
    while surplus > 0:
        candidates = [i for i in range(number_of - 1) if counts[i] < limit]
        whole, budget = sum([portions[i] for i in candidates]), surplus
        for i in candidates:
            more = min(limit - counts[i], max(1, budget * portions[i] // whole), surplus)
            counts[i] = counts[i] + more
            surplus = surplus - more
    return np.array([limit] + counts)


def ragged_sizes(own_key, amount, total, limit, slope):
    if amount == 2:
        one = jax.random.randint(own_key, (), max(1, total - limit), min(limit, total - 1) + 1)
        return jnp.stack([one, total - one])
    lengths = jnp.asarray(split_up(amount, total, limit, slope), jnp.int32)
    twos = (amount - 1) // 2
    source_of, sink = lengths[1:1 + 2 * twos:2], lengths[2:2 + 2 * twos:2]
    slack = jnp.minimum(source_of - 1, limit - sink)
    passed = jax.random.randint(jax.random.fold_in(own_key, 1), (twos,), 0, 1 << 20) % (slack + 1)
    lengths = lengths.at[1:1 + 2 * twos:2].set(source_of - passed).at[2:2 + 2 * twos:2].set(sink + passed)
    return lengths[jax.random.permutation(jax.random.fold_in(own_key, 2), amount)]


def gaussian(own_key, shape, deviation, limit, shards=(), kind=jnp.bfloat16):
    values = jax.random.normal(own_key, shape, jnp.float32) * deviation
    if len(shards) > 0:
        values = block_levels(own_key, shape, shards, -0.22, 0.18) * values
    return jnp.clip(values, min=-limit, max=limit).astype(kind)


def setup_inputs(seed: int = 0) -> dict:
    streams_of = jax.random.split(jax.random.key(seed), 10)
    eig_in = gaussian(streams_of[0], (FF, FF), FF ** -0.5, 0.03125, ((0, 4), (1, 8)))
    eig_out = gaussian(streams_of[1], (D, D), D ** -0.5, 0.0625, ((0, 4), (1, 8)))
    eigvals = draw_eigvals(jax.random.fold_in(streams_of[9], 71), 0)
    out_factors = gaussian(streams_of[3], (D, QCOLS), 0.2, 1.1953125, ((0, 8),))
    in_factors = gaussian(streams_of[4], (FF, QCOLS), 0.2, 1.1953125, ((0, 32),))
    test_matrix = gaussian(streams_of[5], (FF, RANK), FF ** -0.5, 0.03125, ((0, 8),))
    activations = gaussian(streams_of[6], (TOKENS, FF), 1.0, 6.0, ((0, 8), (1, 4)))
    gradients = gaussian(streams_of[7], (TOKENS, D), 0.0001, 0.00059890747, ((0, 8), (1, 4)))
    doc_lengths = ragged_sizes(streams_of[8], DOCUMENTS, TOKENS, DOC_MOST, 2).astype(jnp.int32)
    return dict(eig_in=eig_in, eig_out=eig_out, eigvals=eigvals, out_factors=out_factors, in_factors=in_factors, test_matrix=test_matrix, activations=activations, gradients=gradients, doc_lengths=doc_lengths)


damping = 0.1
highest = lax.Precision.HIGHEST

def reference(eig_in, eig_out, eigvals, out_factors, in_factors, test_matrix, activations, gradients, doc_lengths):
    rot_out = jnp.dot(eig_out.astype(jnp.float32), out_factors.astype(jnp.float32), preferred_element_type=jnp.float32).astype(jnp.bfloat16)
    rot_in = lax.dot_general(eig_in.astype(jnp.float32), in_factors.astype(jnp.float32), (((0,), (0,)), ((), ())), preferred_element_type=jnp.float32).astype(jnp.bfloat16)
    out_split = jnp.transpose(rot_out.reshape(D, QUERIES, LQ), (1, 0, 2))
    in_split = jnp.transpose(rot_in.reshape(FF, QUERIES, LQ), (1, 0, 2))
    test_wide = test_matrix.astype(jnp.float32)

    def one_query(query_pair):
        out_rows, in_rows = query_pair
        weight = 1.0 / (eigvals.astype(jnp.float32) + damping)
        moment = lax.dot_general(out_rows.astype(jnp.float32), in_rows.astype(jnp.float32), (((1,), (1,)), ((), ())), preferred_element_type=jnp.float32) * weight
        sketch = lax.dot_general(test_wide, moment, (((0,), (1,)), ((), ())), precision=highest)
        gram_total = jnp.dot(sketch, sketch.T, precision=highest)
        lower_factor = jnp.linalg.cholesky(gram_total)
        range_rows = lax.linalg.triangular_solve(lower_factor, sketch, left_side=True, lower=True)
        projected = jnp.dot(range_rows, moment, precision=highest).astype(jnp.bfloat16)
        return (range_rows, projected)
    range_all, projected_all = lax.map(one_query, (out_split, in_split))
    right_factor = lax.dot_general(eig_in.astype(jnp.float32), projected_all.reshape(QUERIES * RANK, FF).astype(jnp.float32), (((1,), (1,)), ((), ())), preferred_element_type=jnp.float32).astype(jnp.bfloat16)
    left_factor = lax.dot_general(eig_out.astype(jnp.float32), range_all.reshape(QUERIES * RANK, D), (((0,), (1,)), ((), ())), precision=highest).astype(jnp.bfloat16)
    token_in = jnp.dot(activations.astype(jnp.float32), right_factor.astype(jnp.float32), preferred_element_type=jnp.float32)
    token_out = jnp.dot(gradients.astype(jnp.float32), left_factor.astype(jnp.float32), preferred_element_type=jnp.float32)
    scores = (token_in * token_out).reshape(TOKENS, QUERIES, RANK).sum(axis=2)
    doc_ends = jnp.cumsum(doc_lengths).astype(jnp.int32)
    doc_starts = doc_ends - doc_lengths.astype(jnp.int32)
    positions = jnp.arange(TOKENS, dtype=jnp.int32)
    member = ((positions[:, None] >= doc_starts[None, :]) & (positions[:, None] < doc_ends[None, :])).astype(jnp.float32)
    doc_influence = lax.dot_general(member, scores, (((0,), (0,)), ((), ())), precision=highest)
    return (scores, doc_influence)
```

```python
import functools

import jax
import jax.numpy as jnp
import numpy as np
from jax import lax
from jax.experimental import pallas as pl
from jax.experimental.pallas import tpu as pltpu
from jax.sharding import PartitionSpec as P

QUERIES = 4
LQ = 64
RANK = 32
CORES = 2
GROUPS = 2
RIGHT_PARTS = 2
VMEM = 56 * 1024 * 1024

damping = 0.1
highest = lax.Precision.HIGHEST
f32 = jnp.float32
bf16 = jnp.bfloat16


def tile(extent, most, unit):
    best = extent
    for size in range(unit, min(most, extent) + 1, unit):
        if extent % size == 0:
            best = size
    return best


def params():
    return pltpu.CompilerParams(vmem_limit_bytes=VMEM)


def xor_permute(x, axis, size, bits):
    return lax.ppermute(x, axis, [(i, i ^ bits) for i in range(size)])


def tree_sum(parts):
    while len(parts) > 1:
        parts = [parts[i] + parts[i + 1] for i in range(0, len(parts), 2)]
    return parts[0]


def in_order(parts, me):
    bit = 1
    while bit < len(parts):
        on = (me & bit) != 0
        parts = [jnp.where(on, parts[s ^ bit], parts[s]) for s in range(len(parts))]
        bit *= 2
    return parts


def scatter_direct(x, axis, size, me, unit, dim, kind):
    chunk = x.shape[dim] // size
    total = lax.dynamic_slice_in_dim(x, me * chunk, chunk, dim).astype(f32)
    low = x.astype(kind)
    whole = lax.axis_size(axis)
    for s in range(1, size):
        piece = lax.dynamic_slice_in_dim(low, (me ^ s) * chunk, chunk, dim)
        total = total + xor_permute(piece, axis, whole, unit * s).astype(f32)
    return total


def gather_direct(y, axis, size, me, unit, dim):
    whole = lax.axis_size(axis)
    parts = [y] + [xor_permute(y, axis, whole, unit * s) for s in range(1, size)]
    return jnp.concatenate(in_order(parts, me), axis=dim)


def reduce_basis(x, dim):
    size = lax.axis_size("basis")
    me = lax.axis_index("basis")
    mine = scatter_direct(x, "basis", size, me, 1, dim, bf16).astype(bf16)
    return gather_direct(mine, "basis", size, me, 1, dim)


def halve_basis(x, bits):
    size = lax.axis_size("basis")
    me = lax.axis_index("basis")
    for bit in bits:
        half = x.shape[0] // 2
        on = (me & bit) // bit
        kept = lax.dynamic_slice_in_dim(x, on * half, half, 0)
        given = lax.dynamic_slice_in_dim(x, (1 - on) * half, half, 0)
        x = kept + xor_permute(given, "basis", size, bit)
    x = x.astype(bf16)
    for bit in bits[::-1]:
        on = (me & bit) // bit
        x = jnp.concatenate(in_order([x, xor_permute(x, "basis", size, bit)], on), axis=0)
    return x


def reduce_rotated(x):
    bits = []
    while 1 << len(bits) < lax.axis_size("basis"):
        bits.append(1 << len(bits))
    half = x.shape[0] // 2
    return jnp.concatenate(
        [halve_basis(x[:half], bits), halve_basis(x[half:], bits[::-1])], axis=0
    )


def reduce_docs(x, dim, kind, after=None):
    size = lax.axis_size("docs")
    me = lax.axis_index("docs")
    core, place = me % CORES, me // CORES
    half = x.shape[dim] // CORES
    kept = lax.dynamic_slice_in_dim(x, core * half, half, dim).astype(f32)
    given = lax.dynamic_slice_in_dim(x, (1 - core) * half, half, dim).astype(kind)
    chip = kept + xor_permute(given, "docs", size, 1).astype(f32)
    if after is not None:
        chip, _ = lax.optimization_barrier((chip, after))
    mine = scatter_direct(chip, "docs", size // CORES, place, CORES, dim, kind)
    ours = gather_direct(mine.astype(bf16), "docs", size // CORES, place, CORES, dim)
    theirs = xor_permute(ours, "docs", size, 1)
    return jnp.concatenate(in_order([ours, theirs], core), axis=dim)


def rot_kernel(first, place_ref, factor_ref, eig_ref, *rest):
    out_ref = rest[-1]
    part = jnp.dot(factor_ref[...], eig_ref[...], preferred_element_type=f32)
    if not first:
        part = part + rest[0][...]
    out_ref[...] = part.astype(out_ref.dtype)


def rot_step(place, factors, eig_in, total, dtype):
    rows, depth = factors.shape
    cols = eig_in.shape[1]
    width = tile(cols, 512, 128)
    block = pl.BlockSpec((rows, width), lambda j, place: (0, j))
    specs = [
        pl.BlockSpec((rows, depth), lambda j, place: (0, 0)),
        pl.BlockSpec((depth, width), lambda j, place: (place[0], j)),
    ]
    args = [factors, eig_in]
    if total is not None:
        specs.append(block)
        args.append(total)
    return pl.pallas_call(
        functools.partial(rot_kernel, total is None),
        out_shape=jax.ShapeDtypeStruct((rows, cols), dtype),
        grid_spec=pltpu.PrefetchScalarGridSpec(
            num_scalar_prefetch=1,
            grid=(cols // width,),
            in_specs=specs,
            out_specs=block,
        ),
        compiler_params=params(),
        cost_estimate=pl.CostEstimate(
            flops=2 * rows * depth * cols,
            bytes_accessed=depth * cols * 2 + 2 * rows * cols * 4,
            transcendentals=0,
        ),
        name="rot_step",
    )(place, *args)


def moment_kernel(queries, width, out_ref, in_ref, weight_ref, test_ref, moment_ref, sketch_ref):
    count = len(queries)
    rows, cols = weight_ref.shape
    sides = [out_ref[:, q * LQ : (q + 1) * LQ] for q in queries]

    def step(c, carry):
        at = pl.ds(pl.multiple_of(c * width, width), width)
        weight = weight_ref[:, at]
        for n in range(count):
            product = jnp.dot(
                sides[n], in_ref[n * LQ : (n + 1) * LQ, at], preferred_element_type=f32
            )
            moment_ref[n, :, at] = (product * weight).astype(bf16)
        return carry

    lax.fori_loop(0, cols // width, step, 0)
    sketch = jnp.dot(
        moment_ref[...].reshape(count * rows, cols), test_ref[...], preferred_element_type=f32
    )
    for n in range(count):
        sketch_ref[n * RANK : (n + 1) * RANK, :] = jnp.transpose(
            sketch[n * rows : (n + 1) * rows, :]
        )[:RANK, :]


def moment_pass(queries, rot_out, rot_in, weight, test):
    count = len(queries)
    rows, cols = weight.shape
    height = tile(rows, 256, 128)
    width = tile(cols, 512, 128)
    return pl.pallas_call(
        functools.partial(moment_kernel, queries, width),
        out_shape=(
            jax.ShapeDtypeStruct((count, rows, cols), bf16),
            jax.ShapeDtypeStruct((count * RANK, rows), f32),
        ),
        grid=(rows // height,),
        in_specs=[
            pl.BlockSpec((height, rot_out.shape[1]), lambda i: (i, 0)),
            pl.BlockSpec((count * LQ, cols), lambda i: (0, 0)),
            pl.BlockSpec((height, cols), lambda i: (i, 0)),
            pl.BlockSpec(test.shape, lambda i: (0, 0)),
        ],
        out_specs=(
            pl.BlockSpec((count, height, cols), lambda i: (0, i, 0)),
            pl.BlockSpec((count * RANK, height), lambda i: (0, i)),
        ),
        compiler_params=params(),
        cost_estimate=pl.CostEstimate(
            flops=4 * 2 * count * rows * cols * 256,
            bytes_accessed=count * rows * cols * 2 + rows * cols * 4,
            transcendentals=0,
        ),
        name="moment_pass",
    )(rot_out, rot_in, weight, test)


def cross_kernel(count, sketch_ref, moment_ref, cross_ref):
    for n in range(count):
        cross_ref[n * RANK : (n + 1) * RANK, :] = jnp.dot(
            sketch_ref[n * RANK : (n + 1) * RANK, :], moment_ref[n], preferred_element_type=f32
        )


def cross_pass(sketch, moment):
    count, rows, cols = moment.shape
    width = tile(cols, 256, 128)
    return pl.pallas_call(
        functools.partial(cross_kernel, count),
        out_shape=jax.ShapeDtypeStruct((count * RANK, cols), f32),
        grid=(cols // width,),
        in_specs=[
            pl.BlockSpec(sketch.shape, lambda j: (0, 0)),
            pl.BlockSpec((count, rows, width), lambda j: (0, 0, j)),
        ],
        out_specs=pl.BlockSpec((count * RANK, width), lambda j: (0, j)),
        compiler_params=params(),
        cost_estimate=pl.CostEstimate(
            flops=2 * count * rows * cols * 256,
            bytes_accessed=count * rows * cols * 2,
            transcendentals=0,
        ),
        name="cross_pass",
    )(sketch, moment)


def inverse_kernel(gram_ref, out_ref):
    gram = gram_ref[...]
    row = lax.broadcasted_iota(jnp.int32, gram.shape, 1)
    col = lax.broadcasted_iota(jnp.int32, gram.shape, 2)
    unit = jnp.where(row == col, 1.0, 0.0).astype(f32)
    below = lax.broadcasted_iota(jnp.int32, (gram.shape[0], RANK, 1), 1)
    for k in range(RANK):
        pivot = gram[:, k : k + 1, k : k + 1]
        factor = jnp.where(below > k, gram[:, :, k : k + 1] / pivot, 0.0)
        unit = unit - factor * unit[:, k : k + 1, :]
        gram = gram - factor * gram[:, k : k + 1, :]
    diagonal = jnp.sum(jnp.where(row == col, gram, 0.0), axis=2, keepdims=True)
    out_ref[...] = unit / jnp.sqrt(diagonal)


def inverse_factor(gram):
    return pl.pallas_call(
        inverse_kernel,
        out_shape=jax.ShapeDtypeStruct(gram.shape, f32),
        compiler_params=params(),
        name="inverse_factor",
    )(gram)


def right_kernel(eig_ref, projected_ref, out_ref, across_ref):
    @pl.when(pl.program_id(0) == 0)
    def _():
        across_ref[...] = jnp.transpose(projected_ref[...].astype(f32)).astype(bf16)

    out_ref[...] = jnp.dot(
        eig_ref[...], across_ref[...], preferred_element_type=f32
    ).astype(out_ref.dtype)


def right_pass(eig_in, projected, part, parts):
    rows, cols = eig_in.shape
    rows = rows // parts
    height = tile(rows, 512, 16)
    skip = part * (rows // height)
    return pl.pallas_call(
        right_kernel,
        out_shape=jax.ShapeDtypeStruct((rows, projected.shape[0]), bf16),
        grid=(rows // height,),
        in_specs=[
            pl.BlockSpec((height, cols), lambda i: (i + skip, 0)),
            pl.BlockSpec(projected.shape, lambda i: (0, 0)),
        ],
        out_specs=pl.BlockSpec((height, projected.shape[0]), lambda i: (i, 0)),
        scratch_shapes=[pltpu.VMEM(projected.shape[::-1], bf16)],
        compiler_params=params(),
        cost_estimate=pl.CostEstimate(
            flops=2 * rows * cols * 256,
            bytes_accessed=rows * cols * 2,
            transcendentals=0,
        ),
        name="right_pass",
    )(eig_in, projected)


def rotate_in(eig_in, in_factors):
    size = lax.axis_size("docs")
    places = size // CORES
    me = lax.axis_index("docs")
    core, place = me % CORES, me // CORES
    walk = list(range(0, places, 2)) + list(range(1, places, 2))[::-1]
    after = {walk[p]: walk[(p + 1) % places] for p in range(places)}
    forward = [(z * CORES + c, after[z] * CORES + c) for z in range(places) for c in range(CORES)]
    spot = {z: p for p, z in enumerate(walk)}
    chunk = jnp.transpose(in_factors)
    total = None
    for s in range(places):
        source = jnp.asarray(
            np.array([walk[(spot[z] - s) % places] for z in range(places)], np.int32)
        )[place].reshape(1)
        mate = xor_permute(chunk, "docs", size, 1)
        both = jnp.concatenate(in_order([chunk, mate], core), axis=1)
        last = s == places - 1
        if not last:
            chunk = lax.ppermute(chunk, "docs", forward)
        total = rot_step(source, both, eig_in, total, f32)
    return total, mate


def local(
    eig_in,
    eig_out,
    eigvals,
    out_factors,
    in_factors,
    test_matrix,
    activations,
    gradients,
    doc_lengths,
):
    cols_in = eig_in.shape[1]
    cols_out = eig_out.shape[1]
    tok_count = activations.shape[0]
    basis = lax.axis_size("basis")
    docs = lax.axis_size("docs")

    part_in, arrived = rotate_in(eig_in, in_factors)
    part_out = jnp.dot(eig_out, out_factors, preferred_element_type=f32)
    rot_out = reduce_docs(part_out, 0, f32, after=arrived)
    weight = 1.0 / (eigvals.astype(f32) + damping)

    per = QUERIES // GROUPS
    groups = [tuple(range(g * per, (g + 1) * per)) for g in range(GROUPS)]
    rot_in = [
        reduce_rotated(part_in[g[0] * LQ : (g[-1] + 1) * LQ, :]) for g in groups
    ]
    moments, sketches = [], []
    for n, g in enumerate(groups):
        moment, part = moment_pass(g, rot_out, rot_in[n], weight, test_matrix)
        moments.append(moment)
        sketches.append(part)
    sketches = [reduce_docs(part, 1, f32) for part in sketches]

    projected, lefts = [], []
    for moment, sketch in zip(moments, sketches):
        split = sketch.reshape(per, RANK, sketch.shape[1])
        gram = jnp.einsum("qri,qsi->qrs", split, split, preferred_element_type=f32)
        gram = tree_sum(
            [gram] + [xor_permute(gram, "basis", basis, s) for s in range(1, basis)]
        )
        cross = cross_pass(sketch, moment)
        back = jnp.dot(sketch, eig_out, preferred_element_type=f32)
        inverse = inverse_factor(gram)

        def solve(x):
            x = x.reshape(per, RANK, x.shape[1])
            out = jnp.einsum(
                "qkr,qrj->qkj", inverse, x, precision=highest, preferred_element_type=f32
            )
            return out.reshape(per * RANK, x.shape[2])

        projected.append(reduce_basis(solve(cross), 0))
        lefts.append(solve(back))

    left_block = jnp.transpose(reduce_basis(jnp.concatenate(lefts, axis=0), 0))
    gathered = lax.all_gather(left_block, "docs", axis=0, tiled=True)
    rows_here = gradients.shape[1]
    left_local = lax.dynamic_slice_in_dim(
        gathered, lax.axis_index("basis") * rows_here, rows_here, 0
    )
    token_out = jnp.dot(gradients, left_local, preferred_element_type=f32)

    across = jnp.concatenate(projected, axis=0)
    step = eig_in.shape[0] // RIGHT_PARTS
    rights = [right_pass(eig_in, across, p, RIGHT_PARTS) for p in range(RIGHT_PARTS)]
    token_in = 0.0
    for p, part in enumerate(rights):
        right = reduce_docs(part, 0, bf16)
        token_in = token_in + jnp.dot(
            activations[:, p * step : (p + 1) * step], right, preferred_element_type=f32
        )

    tokens = jnp.concatenate([token_in, token_out], axis=1)
    tokens = tree_sum(
        [tokens] + [xor_permute(tokens, "basis", basis, s) for s in range(1, basis)]
    )
    width = QUERIES * RANK
    scores = (tokens[:, :width] * tokens[:, width:]).reshape(tok_count, QUERIES, RANK).sum(axis=2)
    positions = lax.axis_index("docs") * tok_count + jnp.arange(tok_count, dtype=jnp.int32)
    doc_ends = jnp.cumsum(doc_lengths)
    doc_starts = doc_ends - doc_lengths
    member = (
        (positions[:, None] >= doc_starts[None, :]) & (positions[:, None] < doc_ends[None, :])
    ).astype(f32)
    doc_part = lax.dot_general(member, scores, (((0,), (0,)), ((), ())), precision=highest)
    doc_influence = tree_sum(
        [doc_part] + [xor_permute(doc_part, "docs", docs, s) for s in range(1, docs)]
    )
    return (scores, doc_influence)


def solution(mesh):
    return jax.shard_map(
        local,
        mesh=mesh,
        in_specs=(
            P("basis", "docs"),
            P("basis", "docs"),
            P("basis", "docs"),
            P("docs", None),
            P(("basis", "docs"), None),
            P("docs", None),
            P("docs", "basis"),
            P("docs", "basis"),
            P(),
        ),
        out_specs=(P("docs", None), P()),
        check_vma=False,
    )
```

```python
import functools

import jax
import jax.numpy as jnp
import numpy as np
from jax import lax
from jax.experimental import pallas as pl
from jax.experimental.pallas import tpu as pltpu
from jax.sharding import PartitionSpec as P

QUERIES = 4
LQ = 64
RANK = 32
CORES = 2
VMEM = 56 * 1024 * 1024

damping = 0.1
highest = lax.Precision.HIGHEST
f32 = jnp.float32
bf16 = jnp.bfloat16


def tile(extent, most, unit):
    best = extent
    for size in range(unit, min(most, extent) + 1, unit):
        if extent % size == 0:
            best = size
    return best


def params():
    return pltpu.CompilerParams(vmem_limit_bytes=VMEM)


def xor_permute(x, axis, size, bits):
    return lax.ppermute(x, axis, [(i, i ^ bits) for i in range(size)])


def tree_sum(parts):
    while len(parts) > 1:
        parts = [parts[i] + parts[i + 1] for i in range(0, len(parts), 2)]
    return parts[0]


def in_order(parts, me):
    bit = 1
    while bit < len(parts):
        on = (me & bit) != 0
        parts = [jnp.where(on, parts[s ^ bit], parts[s]) for s in range(len(parts))]
        bit *= 2
    return parts


def scatter_direct(x, axis, size, me, unit, dim, kind):
    chunk = x.shape[dim] // size
    total = lax.dynamic_slice_in_dim(x, me * chunk, chunk, dim).astype(f32)
    low = x.astype(kind)
    whole = lax.axis_size(axis)
    for s in range(1, size):
        piece = lax.dynamic_slice_in_dim(low, (me ^ s) * chunk, chunk, dim)
        total = total + xor_permute(piece, axis, whole, unit * s).astype(f32)
    return total


def gather_direct(y, axis, size, me, unit, dim):
    whole = lax.axis_size(axis)
    parts = [y] + [xor_permute(y, axis, whole, unit * s) for s in range(1, size)]
    return jnp.concatenate(in_order(parts, me), axis=dim)


def reduce_basis(x, dim):
    size = lax.axis_size("basis")
    me = lax.axis_index("basis")
    mine = scatter_direct(x, "basis", size, me, 1, dim, bf16).astype(bf16)
    return gather_direct(mine, "basis", size, me, 1, dim)


def halve_basis(x, bits):
    size = lax.axis_size("basis")
    me = lax.axis_index("basis")
    for n, bit in enumerate(bits):
        half = x.shape[0] // 2
        on = (me & bit) // bit
        kept = lax.dynamic_slice_in_dim(x, on * half, half, 0)
        given = lax.dynamic_slice_in_dim(x, (1 - on) * half, half, 0)
        x = kept + xor_permute(given.astype(f32 if n else bf16), "basis", size, bit).astype(f32)
    x = x.astype(bf16)
    for bit in bits[::-1]:
        on = (me & bit) // bit
        x = jnp.concatenate(in_order([x, xor_permute(x, "basis", size, bit)], on), axis=0)
    return x


def reduce_rotated(x):
    bits = []
    while 1 << len(bits) < lax.axis_size("basis"):
        bits.append(1 << len(bits))
    half = x.shape[0] // 2
    return jnp.concatenate(
        [halve_basis(x[:half], bits), halve_basis(x[half:], bits[::-1])], axis=0
    )


def reduce_docs(x, dim, near, far):
    size = lax.axis_size("docs")
    me = lax.axis_index("docs")
    core, place = me % CORES, me // CORES
    half = x.shape[dim] // CORES
    kept = lax.dynamic_slice_in_dim(x, core * half, half, dim).astype(f32)
    given = lax.dynamic_slice_in_dim(x, (1 - core) * half, half, dim).astype(near)
    chip = kept + xor_permute(given, "docs", size, 1).astype(f32)
    mine = scatter_direct(chip, "docs", size // CORES, place, CORES, dim, far)
    ours = gather_direct(mine.astype(bf16), "docs", size // CORES, place, CORES, dim)
    theirs = xor_permute(ours, "docs", size, 1)
    return jnp.concatenate(in_order([ours, theirs], core), axis=dim)


def moment_kernel(width, out_ref, in_ref, weight_ref, test_ref, *refs):
    moment_refs, sketch_ref = refs[:QUERIES], refs[QUERIES]
    rows, cols = weight_ref.shape
    sides = [out_ref[:, q * LQ : (q + 1) * LQ] for q in range(QUERIES)]

    def step(c, carry):
        at = pl.ds(pl.multiple_of(c * width, width), width)
        weight = weight_ref[:, at]
        for q in range(QUERIES):
            product = jnp.dot(
                sides[q], in_ref[q * LQ : (q + 1) * LQ, at], preferred_element_type=f32
            )
            moment_refs[q][:, at] = (product * weight).astype(bf16)
        return carry

    lax.fori_loop(0, cols // width, step, 0)
    for q in range(QUERIES):
        sketch_ref[q * RANK : (q + 1) * RANK, :] = lax.dot_general(
            test_ref[...],
            moment_refs[q][...],
            (((1,), (1,)), ((), ())),
            preferred_element_type=f32,
        )


def moment_pass(rot_out, rot_in, weight, test):
    rows, cols = weight.shape
    height = tile(rows, 256, 128)
    width = tile(cols, 512, 128)
    *moments, sketch = pl.pallas_call(
        functools.partial(moment_kernel, width),
        out_shape=[jax.ShapeDtypeStruct((rows, cols), bf16)] * QUERIES
        + [jax.ShapeDtypeStruct((QUERIES * RANK, rows), f32)],
        grid=(rows // height,),
        in_specs=[
            pl.BlockSpec((height, rot_out.shape[1]), lambda i: (i, 0)),
            pl.BlockSpec(rot_in.shape, lambda i: (0, 0)),
            pl.BlockSpec((height, cols), lambda i: (i, 0)),
            pl.BlockSpec(test.shape, lambda i: (0, 0)),
        ],
        out_specs=[pl.BlockSpec((height, cols), lambda i: (i, 0))] * QUERIES
        + [pl.BlockSpec((QUERIES * RANK, height), lambda i: (0, i))],
        compiler_params=params(),
        cost_estimate=pl.CostEstimate(
            flops=4 * 2 * QUERIES * rows * cols * 256,
            bytes_accessed=QUERIES * rows * cols * 2 + rows * cols * 4,
            transcendentals=0,
        ),
        name="moment_pass",
    )(rot_out, rot_in, weight, test)
    return moments, sketch


def cross_kernel(sketch_ref, *refs):
    cross_ref = refs[QUERIES]
    for q in range(QUERIES):
        cross_ref[q * RANK : (q + 1) * RANK, :] = jnp.dot(
            sketch_ref[q * RANK : (q + 1) * RANK, :], refs[q][...], preferred_element_type=f32
        )


def cross_pass(sketch, moments):
    rows, cols = moments[0].shape
    width = tile(cols, 512, 128)
    return pl.pallas_call(
        cross_kernel,
        out_shape=jax.ShapeDtypeStruct((QUERIES * RANK, cols), f32),
        grid=(cols // width,),
        in_specs=[pl.BlockSpec(sketch.shape, lambda j: (0, 0))]
        + [pl.BlockSpec((rows, width), lambda j: (0, j))] * QUERIES,
        out_specs=pl.BlockSpec((QUERIES * RANK, width), lambda j: (0, j)),
        compiler_params=params(),
        cost_estimate=pl.CostEstimate(
            flops=2 * QUERIES * rows * cols * 256,
            bytes_accessed=QUERIES * rows * cols * 2,
            transcendentals=0,
        ),
        name="cross_pass",
    )(sketch, *moments)


def inverse_kernel(gram_ref, out_ref):
    gram = gram_ref[...]
    row = lax.broadcasted_iota(jnp.int32, gram.shape, 1)
    col = lax.broadcasted_iota(jnp.int32, gram.shape, 2)
    unit = jnp.where(row == col, 1.0, 0.0).astype(f32)
    below = lax.broadcasted_iota(jnp.int32, (gram.shape[0], RANK, 1), 1)
    for k in range(RANK):
        pivot = gram[:, k : k + 1, k : k + 1]
        factor = jnp.where(below > k, gram[:, :, k : k + 1] / pivot, 0.0)
        unit = unit - factor * unit[:, k : k + 1, :]
        gram = gram - factor * gram[:, k : k + 1, :]
    diagonal = jnp.sum(jnp.where(row == col, gram, 0.0), axis=2, keepdims=True)
    out_ref[...] = unit / jnp.sqrt(diagonal)


def inverse_factor(gram):
    return pl.pallas_call(
        inverse_kernel,
        out_shape=jax.ShapeDtypeStruct(gram.shape, f32),
        compiler_params=params(),
        name="inverse_factor",
    )(gram)


def right_kernel(upper_ref, lower_ref, projected_ref, out_ref, across_ref):
    @pl.when(pl.program_id(0) == 0)
    def _():
        across_ref[...] = jnp.transpose(projected_ref[...].astype(f32)).astype(bf16)

    half = upper_ref.shape[0]
    out_ref[:half, :] = jnp.dot(
        upper_ref[...], across_ref[...], preferred_element_type=f32
    ).astype(out_ref.dtype)
    out_ref[half:, :] = jnp.dot(
        lower_ref[...], across_ref[...], preferred_element_type=f32
    ).astype(out_ref.dtype)


def right_pass(eig_in, projected):
    rows, cols = eig_in.shape
    height = tile(rows // 2, 256, 16)
    width = projected.shape[0]
    return pl.pallas_call(
        right_kernel,
        out_shape=jax.ShapeDtypeStruct((rows, width), bf16),
        grid=(rows // (2 * height),),
        in_specs=[
            pl.BlockSpec((height, cols), lambda i: (2 * i, 0)),
            pl.BlockSpec((height, cols), lambda i: (2 * i + 1, 0)),
            pl.BlockSpec(projected.shape, lambda i: (0, 0)),
        ],
        out_specs=pl.BlockSpec((2 * height, width), lambda i: (i, 0)),
        scratch_shapes=[pltpu.VMEM(projected.shape[::-1], bf16)],
        compiler_params=params(),
        cost_estimate=pl.CostEstimate(
            flops=2 * rows * cols * 256,
            bytes_accessed=rows * cols * 2,
            transcendentals=0,
        ),
        name="right_pass",
    )(eig_in, eig_in, projected)


def rotate_in(eig_in, in_factors):
    size = lax.axis_size("docs")
    places = size // CORES
    me = lax.axis_index("docs")
    core, place = me % CORES, me // CORES
    walk = list(range(0, places, 2)) + list(range(1, places, 2))[::-1]
    after = {walk[p]: walk[(p + 1) % places] for p in range(places)}
    forward = [(z * CORES + c, after[z] * CORES + c) for z in range(places) for c in range(CORES)]
    spot = {z: p for p, z in enumerate(walk)}
    chunk = in_factors
    depth = CORES * in_factors.shape[0]
    total = 0.0
    for s in range(places):
        source = jnp.asarray(
            np.array([walk[(spot[z] - s) % places] for z in range(places)], np.int32)
        )[place]
        mate = xor_permute(chunk, "docs", size, 1)
        both = jnp.concatenate(in_order([chunk, mate], core), axis=0)
        if s < places - 1:
            chunk = lax.ppermute(chunk, "docs", forward)
        rows = lax.dynamic_slice_in_dim(eig_in, source * depth, depth, 0)
        total = total + lax.dot_general(
            both, rows, (((0,), (0,)), ((), ())), preferred_element_type=f32
        )
    return total


def local(
    eig_in,
    eig_out,
    eigvals,
    out_factors,
    in_factors,
    test_matrix,
    activations,
    gradients,
    doc_lengths,
):
    cols_in = eig_in.shape[1]
    tok_count = activations.shape[0]
    basis = lax.axis_size("basis")
    docs = lax.axis_size("docs")

    part_out = jnp.dot(eig_out, out_factors, preferred_element_type=f32)
    rot_out = reduce_docs(part_out, 0, f32, bf16)
    part_in = rotate_in(eig_in, in_factors)
    shift, part_in = lax.optimization_barrier((jnp.float32(damping), part_in))
    weight = 1.0 / (eigvals.astype(f32) + shift)
    rot_in = reduce_rotated(part_in)

    moments, part = moment_pass(rot_out, rot_in, weight, jnp.transpose(test_matrix))
    sketch = reduce_docs(part, 1, f32, f32)
    split = sketch.reshape(QUERIES, RANK, sketch.shape[1])
    gram = jnp.einsum("qri,qsi->qrs", split, split, preferred_element_type=f32)
    gram = tree_sum([gram] + [xor_permute(gram, "basis", basis, s) for s in range(1, basis)])
    cross = cross_pass(sketch, moments)
    back = jnp.dot(sketch, eig_out, preferred_element_type=f32)
    inverse = inverse_factor(gram)
    both = jnp.concatenate([cross, back], axis=1)
    solved = jnp.einsum(
        "qkr,qrj->qkj",
        inverse,
        both.reshape(QUERIES, RANK, both.shape[1]),
        precision=highest,
        preferred_element_type=f32,
    ).reshape(both.shape)
    solved = reduce_basis(solved, 0)
    projected = solved[:, :cols_in]
    left_block = jnp.transpose(solved[:, cols_in:])
    gathered = lax.all_gather(left_block, "docs", axis=0, tiled=True)
    rows_here = gradients.shape[1]
    left_local = lax.dynamic_slice_in_dim(
        gathered, lax.axis_index("basis") * rows_here, rows_here, 0
    )
    token_out = jnp.dot(gradients, left_local, preferred_element_type=f32)
    right = reduce_docs(right_pass(eig_in, projected), 0, bf16, bf16)
    token_in = jnp.dot(activations, right, preferred_element_type=f32)

    tokens = jnp.concatenate([token_in, token_out], axis=1)
    tokens = tree_sum(
        [tokens] + [xor_permute(tokens, "basis", basis, s) for s in range(1, basis)]
    )
    width = QUERIES * RANK
    scores = (tokens[:, :width] * tokens[:, width:]).reshape(tok_count, QUERIES, RANK).sum(axis=2)
    positions = lax.axis_index("docs") * tok_count + jnp.arange(tok_count, dtype=jnp.int32)
    doc_ends = jnp.cumsum(doc_lengths)
    doc_starts = doc_ends - doc_lengths
    member = (
        (positions[:, None] >= doc_starts[None, :]) & (positions[:, None] < doc_ends[None, :])
    ).astype(f32)
    doc_part = lax.dot_general(member, scores, (((0,), (0,)), ((), ())), precision=highest)
    doc_part = doc_part + xor_permute(doc_part, "docs", docs, 1)
    doc_influence = tree_sum(
        [doc_part]
        + [xor_permute(doc_part, "docs", docs, CORES * s) for s in range(1, docs // CORES)]
    )
    return (scores, doc_influence)


def solution(mesh):
    return jax.shard_map(
        local,
        mesh=mesh,
        in_specs=(
            P("basis", "docs"),
            P("basis", "docs"),
            P("basis", "docs"),
            P("docs", None),
            P(("basis", "docs"), None),
            P("docs", None),
            P("docs", "basis"),
            P("docs", "basis"),
            P(),
        ),
        out_specs=(P("docs", None), P()),
        check_vma=False,
    )
```

```python
import functools

import jax
import jax.numpy as jnp
import numpy as np
from jax import lax
from jax.experimental import pallas as pl
from jax.experimental.pallas import tpu as pltpu
from jax.sharding import PartitionSpec as P

QUERIES = 4
LQ = 64
RANK = 32
CORES = 2
VMEM = 56 * 1024 * 1024

damping = 0.1
highest = lax.Precision.HIGHEST
f32 = jnp.float32
bf16 = jnp.bfloat16


def tile(extent, most, unit):
    best = extent
    for size in range(unit, min(most, extent) + 1, unit):
        if extent % size == 0:
            best = size
    return best


def params():
    return pltpu.CompilerParams(vmem_limit_bytes=VMEM)


def hold(x, *others):
    return pl.pallas_call(
        lambda *refs: None,
        out_shape=jax.ShapeDtypeStruct(x.shape, x.dtype),
        in_specs=[pl.BlockSpec(memory_space=pl.ANY)] * (1 + len(others)),
        out_specs=pl.BlockSpec(memory_space=pl.ANY),
        input_output_aliases={0: 0},
        name="hold",
    )(x, *others)


def xor_permute(x, axis, size, bits):
    return lax.ppermute(x, axis, [(i, i ^ bits) for i in range(size)])


def tree_sum(parts):
    while len(parts) > 1:
        parts = [parts[i] + parts[i + 1] for i in range(0, len(parts), 2)]
    return parts[0]


def in_order(parts, me):
    bit = 1
    while bit < len(parts):
        on = (me & bit) != 0
        parts = [jnp.where(on, parts[s ^ bit], parts[s]) for s in range(len(parts))]
        bit *= 2
    return parts


def scatter_direct(x, axis, size, me, unit, dim, kind):
    chunk = x.shape[dim] // size
    total = lax.dynamic_slice_in_dim(x, me * chunk, chunk, dim).astype(f32)
    low = x.astype(kind)
    whole = lax.axis_size(axis)
    for s in range(1, size):
        piece = lax.dynamic_slice_in_dim(low, (me ^ s) * chunk, chunk, dim)
        total = total + xor_permute(piece, axis, whole, unit * s).astype(f32)
    return total


def gather_direct(y, axis, size, me, unit, dim):
    whole = lax.axis_size(axis)
    parts = [y] + [xor_permute(y, axis, whole, unit * s) for s in range(1, size)]
    return jnp.concatenate(in_order(parts, me), axis=dim)


def reduce_basis(x, dim):
    size = lax.axis_size("basis")
    me = lax.axis_index("basis")
    mine = scatter_direct(x, "basis", size, me, 1, dim, bf16).astype(bf16)
    return gather_direct(mine, "basis", size, me, 1, dim)


def halve_basis(x, bits):
    size = lax.axis_size("basis")
    me = lax.axis_index("basis")
    for n, bit in enumerate(bits):
        half = x.shape[0] // 2
        on = (me & bit) // bit
        kept = lax.dynamic_slice_in_dim(x, on * half, half, 0)
        given = lax.dynamic_slice_in_dim(x, (1 - on) * half, half, 0)
        x = kept + xor_permute(given.astype(f32 if n else bf16), "basis", size, bit).astype(f32)
    x = x.astype(bf16)
    for bit in bits[::-1]:
        on = (me & bit) // bit
        x = jnp.concatenate(in_order([x, xor_permute(x, "basis", size, bit)], on), axis=0)
    return x


def reduce_rotated(x):
    bits = []
    while 1 << len(bits) < lax.axis_size("basis"):
        bits.append(1 << len(bits))
    half = x.shape[0] // 2
    return jnp.concatenate(
        [halve_basis(x[:half], bits), halve_basis(x[half:], bits[::-1])], axis=0
    )


def scatter_docs(x, dim, near, far):
    size = lax.axis_size("docs")
    me = lax.axis_index("docs")
    core, place = me % CORES, me // CORES
    half = x.shape[dim] // CORES
    kept = lax.dynamic_slice_in_dim(x, core * half, half, dim).astype(f32)
    given = lax.dynamic_slice_in_dim(x, (1 - core) * half, half, dim).astype(near)
    chip = kept + xor_permute(given, "docs", size, 1).astype(f32)
    return scatter_direct(chip, "docs", size // CORES, place, CORES, dim, far).astype(bf16)


def gather_docs(mine, dim):
    size = lax.axis_size("docs")
    me = lax.axis_index("docs")
    core, place = me % CORES, me // CORES
    ours = gather_direct(mine, "docs", size // CORES, place, CORES, dim)
    theirs = xor_permute(ours, "docs", size, 1)
    return jnp.concatenate(in_order([ours, theirs], core), axis=dim)


def regroup_near(x):
    size = lax.axis_size("docs")
    core = lax.axis_index("docs") % CORES
    half = x.shape[1] // CORES
    kept = lax.dynamic_slice_in_dim(x, core * half, half, 1)
    given = lax.dynamic_slice_in_dim(x, (1 - core) * half, half, 1)
    return jnp.concatenate(in_order([kept, xor_permute(given, "docs", size, 1)], core), axis=0)


def regroup_far(x):
    size = lax.axis_size("docs")
    places = size // CORES
    place = lax.axis_index("docs") // CORES
    chunk = x.shape[1] // places
    parts = [lax.dynamic_slice_in_dim(x, place * chunk, chunk, 1)]
    for s in range(1, places):
        piece = lax.dynamic_slice_in_dim(x, (place ^ s) * chunk, chunk, 1)
        parts.append(xor_permute(piece, "docs", size, CORES * s))
    return parts


def own_tokens(x):
    size = lax.axis_size("docs")
    me = lax.axis_index("docs")
    core, place = me % CORES, me // CORES
    places = size // CORES
    x = x.reshape(places, CORES, x.shape[0] // size, x.shape[1])
    kept = lax.dynamic_index_in_dim(x, core, 1, keepdims=False)
    given = lax.dynamic_index_in_dim(x, 1 - core, 1, keepdims=False)
    chip = kept + xor_permute(given, "docs", size, 1)
    return scatter_direct(chip, "docs", places, place, CORES, 0, f32)[0]


def moment_kernel(width, out_ref, in_ref, values_ref, test_ref, *refs):
    moment_refs, sketch_ref = refs[:QUERIES], refs[QUERIES]
    rows, cols = values_ref.shape
    sides = [out_ref[:, q * LQ : (q + 1) * LQ] for q in range(QUERIES)]

    def step(c, carry):
        at = pl.ds(pl.multiple_of(c * width, width), width)
        weight = 1.0 / (values_ref[:, at].astype(f32) + damping)
        for q in range(QUERIES):
            product = jnp.dot(
                sides[q], in_ref[q * LQ : (q + 1) * LQ, at], preferred_element_type=f32
            )
            moment_refs[q][:, at] = (product * weight).astype(bf16)
        return carry

    lax.fori_loop(0, cols // width, step, 0)
    for q in range(QUERIES):
        sketch_ref[q * RANK : (q + 1) * RANK, :] = lax.dot_general(
            test_ref[...],
            moment_refs[q][...],
            (((1,), (1,)), ((), ())),
            preferred_element_type=f32,
        )


def moment_pass(rot_out, rot_in, eigvals, test):
    rows, cols = eigvals.shape
    height = tile(rows, 256, 128)
    width = tile(cols, 512, 128)
    *moments, sketch = pl.pallas_call(
        functools.partial(moment_kernel, width),
        out_shape=[jax.ShapeDtypeStruct((rows, cols), bf16)] * QUERIES
        + [jax.ShapeDtypeStruct((QUERIES * RANK, rows), f32)],
        grid=(rows // height,),
        in_specs=[
            pl.BlockSpec((height, rot_out.shape[1]), lambda i: (i, 0)),
            pl.BlockSpec(rot_in.shape, lambda i: (0, 0)),
            pl.BlockSpec((height, cols), lambda i: (i, 0)),
            pl.BlockSpec(test.shape, lambda i: (0, 0)),
        ],
        out_specs=[pl.BlockSpec((height, cols), lambda i: (i, 0))] * QUERIES
        + [pl.BlockSpec((QUERIES * RANK, height), lambda i: (0, i))],
        compiler_params=params(),
        cost_estimate=pl.CostEstimate(
            flops=4 * 2 * QUERIES * rows * cols * 256,
            bytes_accessed=QUERIES * rows * cols * 2 + rows * cols * 2,
            transcendentals=0,
        ),
        name="moment_pass",
    )(rot_out, rot_in, eigvals, test)
    return moments, sketch


def cross_kernel(sketch_ref, *refs):
    cross_ref = refs[QUERIES]
    for q in range(QUERIES):
        cross_ref[q * RANK : (q + 1) * RANK, :] = jnp.dot(
            sketch_ref[q * RANK : (q + 1) * RANK, :], refs[q][...], preferred_element_type=f32
        )


def cross_pass(sketch, moments):
    rows, cols = moments[0].shape
    width = tile(cols, 512, 128)
    return pl.pallas_call(
        cross_kernel,
        out_shape=jax.ShapeDtypeStruct((QUERIES * RANK, cols), f32),
        grid=(cols // width,),
        in_specs=[pl.BlockSpec(sketch.shape, lambda j: (0, 0))]
        + [pl.BlockSpec((rows, width), lambda j: (0, j))] * QUERIES,
        out_specs=pl.BlockSpec((QUERIES * RANK, width), lambda j: (0, j)),
        compiler_params=params(),
        cost_estimate=pl.CostEstimate(
            flops=2 * QUERIES * rows * cols * 256,
            bytes_accessed=QUERIES * rows * cols * 2,
            transcendentals=0,
        ),
        name="cross_pass",
    )(sketch, *moments)


def inverse_kernel(gram_ref, out_ref):
    gram = gram_ref[...]
    row = lax.broadcasted_iota(jnp.int32, gram.shape, 1)
    col = lax.broadcasted_iota(jnp.int32, gram.shape, 2)
    unit = jnp.where(row == col, 1.0, 0.0).astype(f32)
    below = lax.broadcasted_iota(jnp.int32, (gram.shape[0], RANK, 1), 1)
    for k in range(RANK):
        pivot = gram[:, k : k + 1, k : k + 1]
        factor = jnp.where(below > k, gram[:, :, k : k + 1] / pivot, 0.0)
        unit = unit - factor * unit[:, k : k + 1, :]
        gram = gram - factor * gram[:, k : k + 1, :]
    diagonal = jnp.sum(jnp.where(row == col, gram, 0.0), axis=2, keepdims=True)
    out_ref[...] = unit / jnp.sqrt(diagonal)


def inverse_factor(gram):
    return pl.pallas_call(
        inverse_kernel,
        out_shape=jax.ShapeDtypeStruct(gram.shape, f32),
        compiler_params=params(),
        name="inverse_factor",
    )(gram)


def right_kernel(parts, *refs):
    projected_ref, out_ref, across_ref = refs[parts:]

    @pl.when(pl.program_id(0) == 0)
    def _():
        across_ref[...] = jnp.transpose(projected_ref[...].astype(f32)).astype(bf16)

    height = refs[0].shape[0]
    for n in range(parts):
        out_ref[n * height : (n + 1) * height, :] = jnp.dot(
            refs[n][...], across_ref[...], preferred_element_type=f32
        ).astype(out_ref.dtype)


def right_pass(eig_in, projected):
    rows, cols = eig_in.shape
    parts = 4
    height = tile(rows // parts, 256, 16)
    width = projected.shape[0]
    return pl.pallas_call(
        functools.partial(right_kernel, parts),
        out_shape=jax.ShapeDtypeStruct((rows, width), bf16),
        grid=(rows // (parts * height),),
        in_specs=[
            pl.BlockSpec((height, cols), lambda i, n=n: (parts * i + n, 0)) for n in range(parts)
        ]
        + [pl.BlockSpec(projected.shape, lambda i: (0, 0))],
        out_specs=pl.BlockSpec((parts * height, width), lambda i: (i, 0)),
        scratch_shapes=[pltpu.VMEM(projected.shape[::-1], bf16)],
        compiler_params=params(),
        cost_estimate=pl.CostEstimate(
            flops=2 * rows * cols * 256,
            bytes_accessed=rows * cols * 2,
            transcendentals=0,
        ),
        name="right_pass",
    )(*[eig_in] * parts, projected)


def rotate_in(eig_in, in_factors, ready):
    size = lax.axis_size("docs")
    places = size // CORES
    me = lax.axis_index("docs")
    core, place = me % CORES, me // CORES
    chunks = [in_factors] + [
        xor_permute(in_factors, "docs", size, CORES * s) for s in range(1, places)
    ]
    depth = CORES * in_factors.shape[0]
    totals = []
    for s, chunk in enumerate(chunks):
        if s > 1:
            chunk = hold(chunk, totals[s - 2])
        mate = xor_permute(chunk, "docs", size, 1)
        if s == places - 1:
            ready = hold(ready, totals[s - 1])
            mate = hold(mate, ready)
        both = jnp.concatenate(in_order([chunk, mate], core), axis=0)
        rows = lax.dynamic_slice_in_dim(eig_in, (place ^ s) * depth, depth, 0)
        product = lax.dot_general(
            both, rows, (((0,), (0,)), ((), ())), preferred_element_type=f32
        )
        totals.append(totals[-1] + product if totals else product)
    return totals[-1], ready


def local(
    eig_in,
    eig_out,
    eigvals,
    out_factors,
    in_factors,
    test_matrix,
    activations,
    gradients,
    doc_lengths,
):
    cols_in = eig_in.shape[1]
    tok_count = activations.shape[0]
    basis = lax.axis_size("basis")
    docs = lax.axis_size("docs")

    part_out = jnp.dot(eig_out, out_factors, preferred_element_type=f32)
    mine_out = scatter_docs(part_out, 0, f32, bf16)
    part_in, mine_out = rotate_in(eig_in, in_factors, mine_out)
    rot_out = gather_docs(hold(mine_out, part_in), 0)
    rot_in = reduce_rotated(part_in)

    moments, part = moment_pass(rot_out, rot_in, eigvals, jnp.transpose(test_matrix))
    all_tokens = regroup_far(hold(regroup_near(activations), rot_in))
    part = hold(part, *[piece[:16, :128] for piece in all_tokens[1:]])
    sketch = gather_docs(scatter_docs(part, 1, f32, bf16), 1)
    split = sketch.reshape(QUERIES, RANK, sketch.shape[1])
    gram = jnp.einsum("qri,qsi->qrs", split, split, preferred_element_type=f32)
    gram = tree_sum([gram] + [xor_permute(gram, "basis", basis, s) for s in range(1, basis)])
    cross = cross_pass(sketch, moments)
    back = jnp.dot(sketch, eig_out, preferred_element_type=f32)
    inverse = inverse_factor(gram)
    both = jnp.concatenate([cross, back], axis=1)
    solved = jnp.einsum(
        "qkr,qrj->qkj",
        inverse,
        both.reshape(QUERIES, RANK, both.shape[1]),
        precision=highest,
        preferred_element_type=f32,
    ).reshape(both.shape)
    solved = reduce_basis(solved, 0)
    projected = solved[:, :cols_in]
    left_block = jnp.transpose(solved[:, cols_in:])
    gathered = lax.all_gather(left_block, "docs", axis=0, tiled=True)
    rows_here = gradients.shape[1]
    left_local = lax.dynamic_slice_in_dim(
        gathered, lax.axis_index("basis") * rows_here, rows_here, 0
    )
    token_out = jnp.dot(gradients, left_local, preferred_element_type=f32)
    right = scatter_docs(right_pass(eig_in, projected), 0, bf16, bf16)
    all_tokens = jnp.concatenate(in_order(all_tokens, lax.axis_index("docs") // CORES), axis=0)
    token_in = own_tokens(jnp.dot(all_tokens, right, preferred_element_type=f32))

    tokens = jnp.concatenate([token_in, token_out], axis=1)
    tokens = tree_sum(
        [tokens] + [xor_permute(tokens, "basis", basis, s) for s in range(1, basis)]
    )
    width = QUERIES * RANK
    scores = (tokens[:, :width] * tokens[:, width:]).reshape(tok_count, QUERIES, RANK).sum(axis=2)
    positions = lax.axis_index("docs") * tok_count + jnp.arange(tok_count, dtype=jnp.int32)
    doc_ends = jnp.cumsum(doc_lengths)
    doc_starts = doc_ends - doc_lengths
    member = (
        (positions[:, None] >= doc_starts[None, :]) & (positions[:, None] < doc_ends[None, :])
    ).astype(f32)
    doc_part = lax.dot_general(member, scores, (((0,), (0,)), ((), ())), precision=highest)
    doc_part = doc_part + xor_permute(doc_part, "docs", docs, 1)
    doc_influence = tree_sum(
        [doc_part]
        + [xor_permute(doc_part, "docs", docs, CORES * s) for s in range(1, docs // CORES)]
    )
    return (scores, doc_influence)


def solution(mesh):
    return jax.shard_map(
        local,
        mesh=mesh,
        in_specs=(
            P("basis", "docs"),
            P("basis", "docs"),
            P("basis", "docs"),
            P("docs", None),
            P(("basis", "docs"), None),
            P("docs", None),
            P("docs", "basis"),
            P("docs", "basis"),
            P(),
        ),
        out_specs=(P("docs", None), P()),
        check_vma=False,
    )
```

```python
import functools

import jax
import jax.numpy as jnp
import numpy as np
from jax import lax
from jax.experimental import pallas as pl
from jax.experimental.pallas import tpu as pltpu
from jax.sharding import PartitionSpec as P

QUERIES = 4
LQ = 64
RANK = 32
CORES = 2
VMEM = 56 * 1024 * 1024

damping = 0.1
highest = lax.Precision.HIGHEST
f32 = jnp.float32
bf16 = jnp.bfloat16


def tile(extent, most, unit):
    best = extent
    for size in range(unit, min(most, extent) + 1, unit):
        if extent % size == 0:
            best = size
    return best


def params():
    return pltpu.CompilerParams(vmem_limit_bytes=VMEM)


def hold(x, *others):
    others = [other[:16, :128] for other in others]
    return pl.pallas_call(
        lambda *refs: None,
        out_shape=jax.ShapeDtypeStruct(x.shape, x.dtype),
        in_specs=[pl.BlockSpec(memory_space=pl.ANY)] * (1 + len(others)),
        out_specs=pl.BlockSpec(memory_space=pl.ANY),
        input_output_aliases={0: 0},
        name="hold",
    )(x, *others)


def xor_permute(x, axis, size, bits):
    return lax.ppermute(x, axis, [(i, i ^ bits) for i in range(size)])


def tree_sum(parts):
    while len(parts) > 1:
        parts = [parts[i] + parts[i + 1] for i in range(0, len(parts), 2)]
    return parts[0]


def in_order(parts, me):
    bit = 1
    while bit < len(parts):
        on = (me & bit) != 0
        parts = [jnp.where(on, parts[s ^ bit], parts[s]) for s in range(len(parts))]
        bit *= 2
    return parts


def scatter_direct(x, axis, size, me, unit, dim, kind):
    chunk = x.shape[dim] // size
    total = lax.dynamic_slice_in_dim(x, me * chunk, chunk, dim).astype(f32)
    low = x.astype(kind)
    whole = lax.axis_size(axis)
    for s in range(1, size):
        piece = lax.dynamic_slice_in_dim(low, (me ^ s) * chunk, chunk, dim)
        total = total + xor_permute(piece, axis, whole, unit * s).astype(f32)
    return total


def gather_direct(y, axis, size, me, unit, dim):
    whole = lax.axis_size(axis)
    parts = [y] + [xor_permute(y, axis, whole, unit * s) for s in range(1, size)]
    return jnp.concatenate(in_order(parts, me), axis=dim)


def reduce_basis(x, dim):
    size = lax.axis_size("basis")
    me = lax.axis_index("basis")
    mine = scatter_direct(x, "basis", size, me, 1, dim, bf16).astype(bf16)
    return gather_direct(mine, "basis", size, me, 1, dim)


def halve_basis(x, bits):
    size = lax.axis_size("basis")
    me = lax.axis_index("basis")
    for n, bit in enumerate(bits):
        half = x.shape[0] // 2
        on = (me & bit) // bit
        kept = lax.dynamic_slice_in_dim(x, on * half, half, 0)
        given = lax.dynamic_slice_in_dim(x, (1 - on) * half, half, 0)
        x = kept + xor_permute(given.astype(f32 if n else bf16), "basis", size, bit).astype(f32)
    x = x.astype(bf16)
    for bit in bits[::-1]:
        on = (me & bit) // bit
        late = x
        x = jnp.concatenate(in_order([x, xor_permute(x, "basis", size, bit)], on), axis=0)
    return x, late


def reduce_rotated(x):
    bits = []
    while 1 << len(bits) < lax.axis_size("basis"):
        bits.append(1 << len(bits))
    half = x.shape[0] // 2
    upper, _ = halve_basis(x[:half], bits)
    lower, late = halve_basis(x[half:], bits[::-1])
    return jnp.concatenate([upper, lower], axis=0), late


def scatter_docs(x, dim, near, far):
    size = lax.axis_size("docs")
    me = lax.axis_index("docs")
    core, place = me % CORES, me // CORES
    half = x.shape[dim] // CORES
    kept = lax.dynamic_slice_in_dim(x, core * half, half, dim).astype(f32)
    given = lax.dynamic_slice_in_dim(x, (1 - core) * half, half, dim).astype(near)
    chip = kept + xor_permute(given, "docs", size, 1).astype(f32)
    return scatter_direct(chip, "docs", size // CORES, place, CORES, dim, far).astype(bf16)


def gather_docs(mine, dim):
    size = lax.axis_size("docs")
    me = lax.axis_index("docs")
    core, place = me % CORES, me // CORES
    ours = gather_direct(mine, "docs", size // CORES, place, CORES, dim)
    theirs = xor_permute(ours, "docs", size, 1)
    return jnp.concatenate(in_order([ours, theirs], core), axis=dim)


def regroup_near(x):
    size = lax.axis_size("docs")
    core = lax.axis_index("docs") % CORES
    half = x.shape[1] // CORES
    kept = lax.dynamic_slice_in_dim(x, core * half, half, 1)
    given = lax.dynamic_slice_in_dim(x, (1 - core) * half, half, 1)
    return jnp.concatenate(in_order([kept, xor_permute(given, "docs", size, 1)], core), axis=0)


def regroup_far(x):
    size = lax.axis_size("docs")
    places = size // CORES
    place = lax.axis_index("docs") // CORES
    chunk = x.shape[1] // places
    parts = [lax.dynamic_slice_in_dim(x, place * chunk, chunk, 1)]
    for s in range(1, places):
        piece = lax.dynamic_slice_in_dim(x, (place ^ s) * chunk, chunk, 1)
        parts.append(xor_permute(piece, "docs", size, CORES * s))
    return parts


def own_tokens(x):
    size = lax.axis_size("docs")
    me = lax.axis_index("docs")
    core, place = me % CORES, me // CORES
    places = size // CORES
    x = x.reshape(places, CORES, x.shape[0] // size, x.shape[1])
    kept = lax.dynamic_index_in_dim(x, core, 1, keepdims=False)
    given = lax.dynamic_index_in_dim(x, 1 - core, 1, keepdims=False)
    chip = kept + xor_permute(given, "docs", size, 1)
    return scatter_direct(chip, "docs", places, place, CORES, 0, f32)[0]


def spread_left(block):
    size = lax.axis_size("docs")
    places = size // CORES
    me = lax.axis_index("docs") // CORES
    here = lax.axis_index("basis")
    left = jnp.where(me == here, block, jnp.zeros_like(block))
    for s in range(1, places):
        pairs = [
            (b * size + b * CORES + c, b * size + (b ^ s) * CORES + c)
            for b in range(places)
            for c in range(CORES)
        ]
        left = left + lax.ppermute(block, ("basis", "docs"), pairs)
    return left


def join_cores(x):
    size = lax.axis_size("docs")
    core = lax.axis_index("docs") % CORES
    return jnp.concatenate(in_order([x, xor_permute(x, "docs", size, 1)], core), axis=1)


def moment_kernel(width, out_ref, in_ref, values_ref, test_ref, *refs):
    moment_refs, sketch_ref = refs[:QUERIES], refs[QUERIES]
    rows, cols = values_ref.shape
    sides = [out_ref[:, q * LQ : (q + 1) * LQ] for q in range(QUERIES)]

    def step(c, carry):
        at = pl.ds(pl.multiple_of(c * width, width), width)
        weight = 1.0 / (values_ref[:, at].astype(f32) + damping)
        for q in range(QUERIES):
            product = jnp.dot(
                sides[q], in_ref[q * LQ : (q + 1) * LQ, at], preferred_element_type=f32
            )
            moment_refs[q][:, at] = (product * weight).astype(bf16)
        return carry

    lax.fori_loop(0, cols // width, step, 0)
    for q in range(QUERIES):
        sketch_ref[q * RANK : (q + 1) * RANK, :] = lax.dot_general(
            test_ref[...],
            moment_refs[q][...],
            (((1,), (1,)), ((), ())),
            preferred_element_type=f32,
        )


def moment_pass(rot_out, rot_in, eigvals, test):
    rows, cols = eigvals.shape
    height = tile(rows, 256, 128)
    width = tile(cols, 512, 128)
    *moments, sketch = pl.pallas_call(
        functools.partial(moment_kernel, width),
        out_shape=[jax.ShapeDtypeStruct((rows, cols), bf16)] * QUERIES
        + [jax.ShapeDtypeStruct((QUERIES * RANK, rows), f32)],
        grid=(rows // height,),
        in_specs=[
            pl.BlockSpec((height, rot_out.shape[1]), lambda i: (i, 0)),
            pl.BlockSpec(rot_in.shape, lambda i: (0, 0)),
            pl.BlockSpec((height, cols), lambda i: (i, 0)),
            pl.BlockSpec(test.shape, lambda i: (0, 0)),
        ],
        out_specs=[pl.BlockSpec((height, cols), lambda i: (i, 0))] * QUERIES
        + [pl.BlockSpec((QUERIES * RANK, height), lambda i: (0, i))],
        compiler_params=params(),
        cost_estimate=pl.CostEstimate(
            flops=4 * 2 * QUERIES * rows * cols * 256,
            bytes_accessed=QUERIES * rows * cols * 2 + rows * cols * 2,
            transcendentals=0,
        ),
        name="moment_pass",
    )(rot_out, rot_in, eigvals, test)
    return moments, sketch


def cross_kernel(sketch_ref, *refs):
    cross_ref = refs[QUERIES]
    for q in range(QUERIES):
        cross_ref[q * RANK : (q + 1) * RANK, :] = jnp.dot(
            sketch_ref[q * RANK : (q + 1) * RANK, :], refs[q][...], preferred_element_type=f32
        )


def cross_pass(sketch, moments):
    rows, cols = moments[0].shape
    width = tile(cols, 512, 128)
    return pl.pallas_call(
        cross_kernel,
        out_shape=jax.ShapeDtypeStruct((QUERIES * RANK, cols), f32),
        grid=(cols // width,),
        in_specs=[pl.BlockSpec(sketch.shape, lambda j: (0, 0))]
        + [pl.BlockSpec((rows, width), lambda j: (0, j))] * QUERIES,
        out_specs=pl.BlockSpec((QUERIES * RANK, width), lambda j: (0, j)),
        compiler_params=params(),
        cost_estimate=pl.CostEstimate(
            flops=2 * QUERIES * rows * cols * 256,
            bytes_accessed=QUERIES * rows * cols * 2,
            transcendentals=0,
        ),
        name="cross_pass",
    )(sketch, *moments)


def inverse_kernel(gram_ref, out_ref):
    gram = gram_ref[...]
    row = lax.broadcasted_iota(jnp.int32, gram.shape, 1)
    col = lax.broadcasted_iota(jnp.int32, gram.shape, 2)
    unit = jnp.where(row == col, 1.0, 0.0).astype(f32)
    below = lax.broadcasted_iota(jnp.int32, (gram.shape[0], RANK, 1), 1)
    for k in range(RANK):
        pivot = gram[:, k : k + 1, k : k + 1]
        factor = jnp.where(below > k, gram[:, :, k : k + 1] / pivot, 0.0)
        unit = unit - factor * unit[:, k : k + 1, :]
        gram = gram - factor * gram[:, k : k + 1, :]
    diagonal = jnp.sum(jnp.where(row == col, gram, 0.0), axis=2, keepdims=True)
    out_ref[...] = unit / jnp.sqrt(diagonal)


def inverse_factor(gram):
    return pl.pallas_call(
        inverse_kernel,
        out_shape=jax.ShapeDtypeStruct(gram.shape, f32),
        compiler_params=params(),
        name="inverse_factor",
    )(gram)


def right_kernel(parts, *refs):
    projected_ref, out_ref, across_ref = refs[parts:]

    @pl.when(pl.program_id(0) == 0)
    def _():
        across_ref[...] = jnp.transpose(projected_ref[...].astype(f32)).astype(bf16)

    height = refs[0].shape[0]
    for n in range(parts):
        out_ref[n * height : (n + 1) * height, :] = jnp.dot(
            refs[n][...], across_ref[...], preferred_element_type=f32
        ).astype(out_ref.dtype)


def right_pass(eig_in, projected):
    rows, cols = eig_in.shape
    parts = 4
    height = tile(rows // parts, 256, 16)
    width = projected.shape[0]
    return pl.pallas_call(
        functools.partial(right_kernel, parts),
        out_shape=jax.ShapeDtypeStruct((rows, width), bf16),
        grid=(rows // (parts * height),),
        in_specs=[
            pl.BlockSpec((height, cols), lambda i, n=n: (parts * i + n, 0)) for n in range(parts)
        ]
        + [pl.BlockSpec(projected.shape, lambda i: (0, 0))],
        out_specs=pl.BlockSpec((parts * height, width), lambda i: (i, 0)),
        scratch_shapes=[pltpu.VMEM(projected.shape[::-1], bf16)],
        compiler_params=params(),
        cost_estimate=pl.CostEstimate(
            flops=2 * rows * cols * 256,
            bytes_accessed=rows * cols * 2,
            transcendentals=0,
        ),
        name="right_pass",
    )(*[eig_in] * parts, projected)


def rotate_in(eig_in, in_factors, ready):
    size = lax.axis_size("docs")
    places = size // CORES
    me = lax.axis_index("docs")
    core, place = me % CORES, me // CORES
    chunks = [in_factors]
    depth = CORES * in_factors.shape[0]
    totals = []
    for s in range(places):
        if s > 0:
            low = s & -s
            chunks.append(xor_permute(chunks[s - low], "docs", size, CORES * low))
    for s, chunk in enumerate(chunks):
        if s > 1:
            chunk = hold(chunk, totals[1])
        mate = xor_permute(chunk, "docs", size, 1)
        if s == places - 1:
            ready = hold(ready, totals[s - 1])
            mate = hold(mate, ready)
        both = jnp.concatenate(in_order([chunk, mate], core), axis=0)
        rows = lax.dynamic_slice_in_dim(eig_in, (place ^ s) * depth, depth, 0)
        product = lax.dot_general(
            both, rows, (((0,), (0,)), ((), ())), preferred_element_type=f32
        )
        totals.append(totals[-1] + product if totals else product)
    return totals[-1], ready


def local(
    eig_in,
    eig_out,
    eigvals,
    out_factors,
    in_factors,
    test_matrix,
    activations,
    gradients,
    doc_lengths,
):
    cols_in = eig_in.shape[1]
    tok_count = activations.shape[0]
    basis = lax.axis_size("basis")
    docs = lax.axis_size("docs")

    part_out = jnp.dot(eig_out, out_factors, preferred_element_type=f32)
    mine_out = scatter_docs(part_out, 0, f32, bf16)
    part_in, mine_out = rotate_in(eig_in, in_factors, mine_out)
    rot_out = gather_docs(hold(mine_out, part_in), 0)
    rot_in, late = reduce_rotated(part_in)

    moments, part = moment_pass(rot_out, rot_in, eigvals, jnp.transpose(test_matrix))
    all_tokens = regroup_far(hold(regroup_near(activations), late))
    part = hold(part, *all_tokens[1:])
    sketch = gather_docs(scatter_docs(part, 1, f32, bf16), 1)
    split = sketch.reshape(QUERIES, RANK, sketch.shape[1])
    gram = jnp.einsum("qri,qsi->qrs", split, split, preferred_element_type=f32)
    gram = tree_sum([gram] + [xor_permute(gram, "basis", basis, s) for s in range(1, basis)])
    cross = cross_pass(sketch, moments)
    back = jnp.dot(sketch, eig_out, preferred_element_type=f32)
    inverse = inverse_factor(gram)
    both = jnp.concatenate([cross, back], axis=1)
    solved = jnp.einsum(
        "qkr,qrj->qkj",
        inverse,
        both.reshape(QUERIES, RANK, both.shape[1]),
        precision=highest,
        preferred_element_type=f32,
    ).reshape(both.shape)
    solved = reduce_basis(solved, 0)
    projected = solved[:, :cols_in]
    left = spread_left(solved[:, cols_in:])
    right = hold(right_pass(eig_in, projected), left)
    token_out = lax.dot_general(
        gradients, join_cores(left), (((1,), (1,)), ((), ())), preferred_element_type=f32
    )
    right = scatter_docs(right, 0, bf16, bf16)
    all_tokens = jnp.concatenate(in_order(all_tokens, lax.axis_index("docs") // CORES), axis=0)
    token_in = own_tokens(jnp.dot(all_tokens, right, preferred_element_type=f32))

    tokens = jnp.concatenate([token_in, token_out], axis=1)
    tokens = tree_sum(
        [tokens] + [xor_permute(tokens, "basis", basis, s) for s in range(1, basis)]
    )
    width = QUERIES * RANK
    scores = (tokens[:, :width] * tokens[:, width:]).reshape(tok_count, QUERIES, RANK).sum(axis=2)
    positions = lax.axis_index("docs") * tok_count + jnp.arange(tok_count, dtype=jnp.int32)
    doc_ends = jnp.cumsum(doc_lengths)
    doc_starts = doc_ends - doc_lengths
    member = (
        (positions[:, None] >= doc_starts[None, :]) & (positions[:, None] < doc_ends[None, :])
    ).astype(f32)
    doc_part = lax.dot_general(member, scores, (((0,), (0,)), ((), ())), precision=highest)
    doc_part = doc_part + xor_permute(doc_part, "docs", docs, 1)
    doc_influence = tree_sum(
        [doc_part]
        + [xor_permute(doc_part, "docs", docs, CORES * s) for s in range(1, docs // CORES)]
    )
    return (scores, doc_influence)


def solution(mesh):
    return jax.shard_map(
        local,
        mesh=mesh,
        in_specs=(
            P("basis", "docs"),
            P("basis", "docs"),
            P("basis", "docs"),
            P("docs", None),
            P(("basis", "docs"), None),
            P("docs", None),
            P("docs", "basis"),
            P("docs", "basis"),
            P(),
        ),
        out_specs=(P("docs", None), P()),
        check_vma=False,
    )
```

```python
import functools

import jax
import jax.numpy as jnp
import numpy as np
from jax import lax
from jax.experimental import pallas as pl
from jax.experimental.pallas import tpu as pltpu
from jax.sharding import PartitionSpec as P

QUERIES = 4
LQ = 64
RANK = 32
CORES = 2
VMEM = 56 * 1024 * 1024

damping = 0.1
highest = lax.Precision.HIGHEST
f32 = jnp.float32
bf16 = jnp.bfloat16


def tile(extent, most, unit):
    best = extent
    for size in range(unit, min(most, extent) + 1, unit):
        if extent % size == 0:
            best = size
    return best


def params():
    return pltpu.CompilerParams(vmem_limit_bytes=VMEM)


def hold(x, *others):
    other = sum(other[:16, :128].astype(f32) for other in others)
    return pl.pallas_call(
        lambda *refs: None,
        out_shape=jax.ShapeDtypeStruct(x.shape, x.dtype),
        in_specs=[pl.BlockSpec(memory_space=pl.ANY)] * 2,
        out_specs=pl.BlockSpec(memory_space=pl.ANY),
        input_output_aliases={0: 0},
        name="hold",
    )(x, other)


def xor_permute(x, axis, size, bits):
    return lax.ppermute(x, axis, [(i, i ^ bits) for i in range(size)])


def tree_sum(parts):
    while len(parts) > 1:
        parts = [parts[i] + parts[i + 1] for i in range(0, len(parts), 2)]
    return parts[0]


def in_order(parts, me):
    bit = 1
    while bit < len(parts):
        on = (me & bit) != 0
        parts = [jnp.where(on, parts[s ^ bit], parts[s]) for s in range(len(parts))]
        bit *= 2
    return parts


def scatter_direct(x, axis, size, me, unit, dim, kind):
    chunk = x.shape[dim] // size
    total = lax.dynamic_slice_in_dim(x, me * chunk, chunk, dim).astype(f32)
    low = x.astype(kind)
    whole = lax.axis_size(axis)
    for s in range(1, size):
        piece = lax.dynamic_slice_in_dim(low, (me ^ s) * chunk, chunk, dim)
        total = total + xor_permute(piece, axis, whole, unit * s).astype(f32)
    return total


def gather_direct(y, axis, size, me, unit, dim):
    whole = lax.axis_size(axis)
    parts = [y] + [xor_permute(y, axis, whole, unit * s) for s in range(1, size)]
    return jnp.concatenate(in_order(parts, me), axis=dim)


def reduce_basis(x, dim):
    size = lax.axis_size("basis")
    me = lax.axis_index("basis")
    mine = scatter_direct(x, "basis", size, me, 1, dim, bf16).astype(bf16)
    return gather_direct(mine, "basis", size, me, 1, dim)


def halve_basis(x, bits):
    size = lax.axis_size("basis")
    me = lax.axis_index("basis")
    for n, bit in enumerate(bits):
        half = x.shape[0] // 2
        on = (me & bit) // bit
        kept = lax.dynamic_slice_in_dim(x, on * half, half, 0)
        given = lax.dynamic_slice_in_dim(x, (1 - on) * half, half, 0)
        x = kept + xor_permute(given.astype(f32 if n else bf16), "basis", size, bit).astype(f32)
        if n == 0:
            early = x
    x = x.astype(bf16)
    for bit in bits[::-1]:
        on = (me & bit) // bit
        late = x
        x = jnp.concatenate(in_order([x, xor_permute(x, "basis", size, bit)], on), axis=0)
    return x, early, late


def reduce_rotated(x):
    bits = []
    while 1 << len(bits) < lax.axis_size("basis"):
        bits.append(1 << len(bits))
    half = x.shape[0] // 2
    upper, *upper_marks = halve_basis(x[:half], bits)
    lower, *lower_marks = halve_basis(x[half:], bits[::-1])
    return jnp.concatenate([upper, lower], axis=0), list(zip(upper_marks, lower_marks))


def scatter_docs(x, dim, near, far, after=None):
    size = lax.axis_size("docs")
    me = lax.axis_index("docs")
    core, place = me % CORES, me // CORES
    half = x.shape[dim] // CORES
    kept = lax.dynamic_slice_in_dim(x, core * half, half, dim).astype(f32)
    given = lax.dynamic_slice_in_dim(x, (1 - core) * half, half, dim).astype(near)
    chip = kept + xor_permute(given, "docs", size, 1).astype(f32)
    if after is not None:
        chip = hold(chip, after)
    return scatter_direct(chip, "docs", size // CORES, place, CORES, dim, far).astype(bf16)


def gather_docs(mine, dim):
    size = lax.axis_size("docs")
    me = lax.axis_index("docs")
    core, place = me % CORES, me // CORES
    ours = gather_direct(mine, "docs", size // CORES, place, CORES, dim)
    theirs = xor_permute(ours, "docs", size, 1)
    return jnp.concatenate(in_order([ours, theirs], core), axis=dim)


def regroup_near(x):
    size = lax.axis_size("docs")
    core = lax.axis_index("docs") % CORES
    half = x.shape[1] // CORES
    kept = lax.dynamic_slice_in_dim(x, core * half, half, 1)
    given = lax.dynamic_slice_in_dim(x, (1 - core) * half, half, 1)
    return jnp.concatenate(in_order([kept, xor_permute(given, "docs", size, 1)], core), axis=0)


def regroup_far(x):
    size = lax.axis_size("docs")
    places = size // CORES
    place = lax.axis_index("docs") // CORES
    chunk = x.shape[1] // places
    parts = [lax.dynamic_slice_in_dim(x, place * chunk, chunk, 1)]
    for s in range(1, places):
        piece = lax.dynamic_slice_in_dim(x, (place ^ s) * chunk, chunk, 1)
        parts.append(xor_permute(piece, "docs", size, CORES * s))
    return parts


def own_tokens(x):
    size = lax.axis_size("docs")
    me = lax.axis_index("docs")
    core, place = me % CORES, me // CORES
    places = size // CORES
    x = x.reshape(places, CORES, x.shape[0] // size, x.shape[1])
    kept = lax.dynamic_index_in_dim(x, core, 1, keepdims=False)
    given = lax.dynamic_index_in_dim(x, 1 - core, 1, keepdims=False)
    chip = kept + xor_permute(given, "docs", size, 1)
    return scatter_direct(chip, "docs", places, place, CORES, 0, f32)[0]


def spread_left(block):
    size = lax.axis_size("docs")
    places = size // CORES
    me = lax.axis_index("docs") // CORES
    here = lax.axis_index("basis")
    left = jnp.where(me == here, block, jnp.zeros_like(block))
    for s in range(1, places):
        pairs = [
            (b * size + b * CORES + c, b * size + (b ^ s) * CORES + c)
            for b in range(places)
            for c in range(CORES)
        ]
        left = left + lax.ppermute(block, ("basis", "docs"), pairs)
    return left


def join_cores(x):
    size = lax.axis_size("docs")
    core = lax.axis_index("docs") % CORES
    return jnp.concatenate(in_order([x, xor_permute(x, "docs", size, 1)], core), axis=1)


def moment_kernel(width, out_ref, in_ref, values_ref, test_ref, *refs):
    moment_refs, sketch_ref = refs[:QUERIES], refs[QUERIES]
    rows, cols = values_ref.shape
    sides = [out_ref[:, q * LQ : (q + 1) * LQ] for q in range(QUERIES)]

    sketch_ref[...] = jnp.zeros_like(sketch_ref)

    def step(c, carry):
        at = pl.ds(pl.multiple_of(c * width, width), width)
        weight = 1.0 / (values_ref[:, at].astype(f32) + damping)
        for q in range(QUERIES):
            product = jnp.dot(
                sides[q], in_ref[q * LQ : (q + 1) * LQ, at], preferred_element_type=f32
            )
            moment = (product * weight).astype(bf16)
            moment_refs[q][:, at] = moment
            sketch_ref[q * RANK : (q + 1) * RANK, :] += lax.dot_general(
                test_ref[:, at], moment, (((1,), (1,)), ((), ())), preferred_element_type=f32
            )
        return carry

    lax.fori_loop(0, cols // width, step, 0)


def moment_pass(rot_out, rot_in, eigvals, test):
    rows, cols = eigvals.shape
    height = tile(rows, 256, 128)
    width = tile(cols, 512, 128)
    *moments, sketch = pl.pallas_call(
        functools.partial(moment_kernel, width),
        out_shape=[jax.ShapeDtypeStruct((rows, cols), bf16)] * QUERIES
        + [jax.ShapeDtypeStruct((QUERIES * RANK, rows), f32)],
        grid=(rows // height,),
        in_specs=[
            pl.BlockSpec((height, rot_out.shape[1]), lambda i: (i, 0)),
            pl.BlockSpec(rot_in.shape, lambda i: (0, 0)),
            pl.BlockSpec((height, cols), lambda i: (i, 0)),
            pl.BlockSpec(test.shape, lambda i: (0, 0)),
        ],
        out_specs=[pl.BlockSpec((height, cols), lambda i: (i, 0))] * QUERIES
        + [pl.BlockSpec((QUERIES * RANK, height), lambda i: (0, i))],
        compiler_params=params(),
        cost_estimate=pl.CostEstimate(
            flops=4 * 2 * QUERIES * rows * cols * 256,
            bytes_accessed=QUERIES * rows * cols * 2 + rows * cols * 2,
            transcendentals=0,
        ),
        name="moment_pass",
    )(rot_out, rot_in, eigvals, test)
    return moments, sketch


def cross_kernel(sketch_ref, *refs):
    cross_ref = refs[QUERIES]
    for q in range(QUERIES):
        cross_ref[q * RANK : (q + 1) * RANK, :] = jnp.dot(
            sketch_ref[q * RANK : (q + 1) * RANK, :], refs[q][...], preferred_element_type=f32
        )


def cross_pass(sketch, moments):
    rows, cols = moments[0].shape
    width = tile(cols, 512, 128)
    return pl.pallas_call(
        cross_kernel,
        out_shape=jax.ShapeDtypeStruct((QUERIES * RANK, cols), f32),
        grid=(cols // width,),
        in_specs=[pl.BlockSpec(sketch.shape, lambda j: (0, 0))]
        + [pl.BlockSpec((rows, width), lambda j: (0, j))] * QUERIES,
        out_specs=pl.BlockSpec((QUERIES * RANK, width), lambda j: (0, j)),
        compiler_params=params(),
        cost_estimate=pl.CostEstimate(
            flops=2 * QUERIES * rows * cols * 256,
            bytes_accessed=QUERIES * rows * cols * 2,
            transcendentals=0,
        ),
        name="cross_pass",
    )(sketch, *moments)


def inverse_kernel(gram_ref, out_ref):
    gram = gram_ref[...]
    row = lax.broadcasted_iota(jnp.int32, gram.shape, 1)
    col = lax.broadcasted_iota(jnp.int32, gram.shape, 2)
    unit = jnp.where(row == col, 1.0, 0.0).astype(f32)
    below = lax.broadcasted_iota(jnp.int32, (gram.shape[0], RANK, 1), 1)
    for k in range(RANK):
        pivot = gram[:, k : k + 1, k : k + 1]
        factor = jnp.where(below > k, gram[:, :, k : k + 1] / pivot, 0.0)
        unit = unit - factor * unit[:, k : k + 1, :]
        gram = gram - factor * gram[:, k : k + 1, :]
    diagonal = jnp.sum(jnp.where(row == col, gram, 0.0), axis=2, keepdims=True)
    out_ref[...] = unit / jnp.sqrt(diagonal)


def inverse_factor(gram):
    return pl.pallas_call(
        inverse_kernel,
        out_shape=jax.ShapeDtypeStruct(gram.shape, f32),
        compiler_params=params(),
        name="inverse_factor",
    )(gram)


def right_kernel(parts, *refs):
    projected_ref, out_ref, across_ref = refs[parts:]

    @pl.when(pl.program_id(0) == 0)
    def _():
        across_ref[...] = jnp.transpose(projected_ref[...].astype(f32)).astype(bf16)

    height = refs[0].shape[0]
    for n in range(parts):
        out_ref[n * height : (n + 1) * height, :] = jnp.dot(
            refs[n][...], across_ref[...], preferred_element_type=f32
        ).astype(out_ref.dtype)


def right_pass(eig_in, projected):
    rows, cols = eig_in.shape
    parts = 4
    height = tile(rows // parts, 256, 16)
    width = projected.shape[0]
    return pl.pallas_call(
        functools.partial(right_kernel, parts),
        out_shape=jax.ShapeDtypeStruct((rows, width), bf16),
        grid=(rows // (parts * height),),
        in_specs=[
            pl.BlockSpec((height, cols), lambda i, n=n: (parts * i + n, 0)) for n in range(parts)
        ]
        + [pl.BlockSpec(projected.shape, lambda i: (0, 0))],
        out_specs=pl.BlockSpec((parts * height, width), lambda i: (i, 0)),
        scratch_shapes=[pltpu.VMEM(projected.shape[::-1], bf16)],
        compiler_params=params(),
        cost_estimate=pl.CostEstimate(
            flops=2 * rows * cols * 256,
            bytes_accessed=rows * cols * 2,
            transcendentals=0,
        ),
        name="right_pass",
    )(*[eig_in] * parts, projected)


def rotate_in(eig_in, in_factors):
    size = lax.axis_size("docs")
    places = size // CORES
    me = lax.axis_index("docs")
    core, place = me % CORES, me // CORES
    chunks = [in_factors]
    depth = CORES * in_factors.shape[0]
    totals = []
    for s in range(places):
        if s > 0:
            low = s & -s
            chunks.append(xor_permute(chunks[s - low], "docs", size, CORES * low))
    for s, chunk in enumerate(chunks):
        if s & (s - 1):
            chunk = hold(chunk, totals[1])
        mate = xor_permute(chunk, "docs", size, 1)
        both = jnp.concatenate(in_order([chunk, mate], core), axis=0)
        rows = lax.dynamic_slice_in_dim(eig_in, (place ^ s) * depth, depth, 0)
        product = lax.dot_general(
            both, rows, (((0,), (0,)), ((), ())), preferred_element_type=f32
        )
        totals.append(totals[-1] + product if totals else product)
    return totals[-1]


def local(
    eig_in,
    eig_out,
    eigvals,
    out_factors,
    in_factors,
    test_matrix,
    activations,
    gradients,
    doc_lengths,
):
    cols_in = eig_in.shape[1]
    tok_count = activations.shape[0]
    basis = lax.axis_size("basis")
    docs = lax.axis_size("docs")

    part_out = jnp.dot(eig_out, out_factors, preferred_element_type=f32)
    part_in = rotate_in(eig_in, in_factors)
    rot_in, (early, late) = reduce_rotated(part_in)
    rot_out = scatter_docs(part_out, 0, f32, bf16, after=part_in)
    rot_out = gather_docs(hold(rot_out, *early), 0)

    moments, part = moment_pass(rot_out, rot_in, eigvals, jnp.transpose(test_matrix))
    all_tokens = regroup_far(hold(regroup_near(activations), late[1]))
    part = hold(part, *all_tokens[1:])
    sketch = gather_docs(scatter_docs(part, 1, f32, bf16), 1)
    split = sketch.reshape(QUERIES, RANK, sketch.shape[1])
    gram = jnp.einsum("qri,qsi->qrs", split, split, preferred_element_type=f32)
    gram = tree_sum([gram] + [xor_permute(gram, "basis", basis, s) for s in range(1, basis)])
    cross = cross_pass(sketch, moments)
    back = jnp.dot(sketch, eig_out, preferred_element_type=f32)
    inverse = inverse_factor(gram)
    both = jnp.concatenate([cross, back], axis=1)
    solved = jnp.einsum(
        "qkr,qrj->qkj",
        inverse,
        both.reshape(QUERIES, RANK, both.shape[1]),
        precision=highest,
        preferred_element_type=f32,
    ).reshape(both.shape)
    solved = reduce_basis(solved, 0)
    projected = solved[:, :cols_in]
    left = spread_left(solved[:, cols_in:])
    right = hold(right_pass(eig_in, projected), left)
    token_out = lax.dot_general(
        gradients, join_cores(left), (((1,), (1,)), ((), ())), preferred_element_type=f32
    )
    right = scatter_docs(right, 0, bf16, bf16)
    all_tokens = jnp.concatenate(in_order(all_tokens, lax.axis_index("docs") // CORES), axis=0)
    token_in = own_tokens(jnp.dot(all_tokens, right, preferred_element_type=f32))

    tokens = jnp.concatenate([token_in, token_out], axis=1)
    tokens = tree_sum(
        [tokens] + [xor_permute(tokens, "basis", basis, s) for s in range(1, basis)]
    )
    width = QUERIES * RANK
    scores = (tokens[:, :width] * tokens[:, width:]).reshape(tok_count, QUERIES, RANK).sum(axis=2)
    positions = lax.axis_index("docs") * tok_count + jnp.arange(tok_count, dtype=jnp.int32)
    doc_ends = jnp.cumsum(doc_lengths)
    doc_starts = doc_ends - doc_lengths
    member = (
        (positions[:, None] >= doc_starts[None, :]) & (positions[:, None] < doc_ends[None, :])
    ).astype(f32)
    doc_part = lax.dot_general(member, scores, (((0,), (0,)), ((), ())), precision=highest)
    doc_part = doc_part + xor_permute(doc_part, "docs", docs, 1)
    doc_influence = tree_sum(
        [doc_part]
        + [xor_permute(doc_part, "docs", docs, CORES * s) for s in range(1, docs // CORES)]
    )
    return (scores, doc_influence)


def solution(mesh):
    return jax.shard_map(
        local,
        mesh=mesh,
        in_specs=(
            P("basis", "docs"),
            P("basis", "docs"),
            P("basis", "docs"),
            P("docs", None),
            P(("basis", "docs"), None),
            P("docs", None),
            P("docs", "basis"),
            P("docs", "basis"),
            P(),
        ),
        out_specs=(P("docs", None), P()),
        check_vma=False,
    )
```

```python
import functools

import jax
import jax.numpy as jnp
import numpy as np
from jax import lax
from jax.experimental import pallas as pl
from jax.experimental.pallas import tpu as pltpu
from jax.sharding import PartitionSpec as P

QUERIES = 4
LQ = 64
RANK = 32
CORES = 2
VMEM = 56 * 1024 * 1024

damping = 0.1
highest = lax.Precision.HIGHEST
f32 = jnp.float32
bf16 = jnp.bfloat16


def tile(extent, most, unit):
    best = extent
    for size in range(unit, min(most, extent) + 1, unit):
        if extent % size == 0:
            best = size
    return best


def params():
    return pltpu.CompilerParams(vmem_limit_bytes=VMEM)


def hold(x, *others):
    other = sum(other[:16, :128].astype(f32) for other in others)
    return pl.pallas_call(
        lambda *refs: None,
        out_shape=jax.ShapeDtypeStruct(x.shape, x.dtype),
        in_specs=[pl.BlockSpec(memory_space=pl.ANY)] * 2,
        out_specs=pl.BlockSpec(memory_space=pl.ANY),
        input_output_aliases={0: 0},
        name="hold",
    )(x, other)


def xor_permute(x, axis, size, bits):
    return lax.ppermute(x, axis, [(i, i ^ bits) for i in range(size)])


def tree_sum(parts):
    while len(parts) > 1:
        parts = [parts[i] + parts[i + 1] for i in range(0, len(parts), 2)]
    return parts[0]


def in_order(parts, me):
    bit = 1
    while bit < len(parts):
        on = (me & bit) != 0
        parts = [jnp.where(on, parts[s ^ bit], parts[s]) for s in range(len(parts))]
        bit *= 2
    return parts


def scatter_direct(x, axis, size, me, unit, dim, kind):
    chunk = x.shape[dim] // size
    total = lax.dynamic_slice_in_dim(x, me * chunk, chunk, dim).astype(f32)
    low = x.astype(kind)
    whole = lax.axis_size(axis)
    for s in range(1, size):
        piece = lax.dynamic_slice_in_dim(low, (me ^ s) * chunk, chunk, dim)
        total = total + xor_permute(piece, axis, whole, unit * s).astype(f32)
    return total


def gather_direct(y, axis, size, me, unit, dim):
    whole = lax.axis_size(axis)
    parts = [y] + [xor_permute(y, axis, whole, unit * s) for s in range(1, size)]
    return jnp.concatenate(in_order(parts, me), axis=dim)


def reduce_basis(x, dim):
    size = lax.axis_size("basis")
    me = lax.axis_index("basis")
    mine = scatter_direct(x, "basis", size, me, 1, dim, bf16).astype(bf16)
    return gather_direct(mine, "basis", size, me, 1, dim)


def halve_basis(x, bits):
    size = lax.axis_size("basis")
    me = lax.axis_index("basis")
    for n, bit in enumerate(bits):
        half = x.shape[0] // 2
        on = (me & bit) // bit
        kept = lax.dynamic_slice_in_dim(x, on * half, half, 0)
        given = lax.dynamic_slice_in_dim(x, (1 - on) * half, half, 0)
        x = kept + xor_permute(given.astype(f32 if n else bf16), "basis", size, bit).astype(f32)
        if n == 0:
            early = x
    x = x.astype(bf16)
    for bit in bits[::-1]:
        on = (me & bit) // bit
        late = x
        x = jnp.concatenate(in_order([x, xor_permute(x, "basis", size, bit)], on), axis=0)
    return x, early, late


def reduce_rotated(x):
    bits = []
    while 1 << len(bits) < lax.axis_size("basis"):
        bits.append(1 << len(bits))
    half = x.shape[0] // 2
    upper, *upper_marks = halve_basis(x[:half], bits)
    lower, *lower_marks = halve_basis(x[half:], bits[::-1])
    return jnp.concatenate([upper, lower], axis=0), list(zip(upper_marks, lower_marks))


def scatter_docs(x, dim, near, far, after=None):
    size = lax.axis_size("docs")
    me = lax.axis_index("docs")
    core, place = me % CORES, me // CORES
    half = x.shape[dim] // CORES
    kept = lax.dynamic_slice_in_dim(x, core * half, half, dim).astype(f32)
    given = lax.dynamic_slice_in_dim(x, (1 - core) * half, half, dim).astype(near)
    chip = kept + xor_permute(given, "docs", size, 1).astype(f32)
    if after is not None:
        chip = hold(chip, after)
    return scatter_direct(chip, "docs", size // CORES, place, CORES, dim, far).astype(bf16)


def gather_docs(mine, dim):
    size = lax.axis_size("docs")
    me = lax.axis_index("docs")
    core, place = me % CORES, me // CORES
    ours = gather_direct(mine, "docs", size // CORES, place, CORES, dim)
    theirs = xor_permute(ours, "docs", size, 1)
    return jnp.concatenate(in_order([ours, theirs], core), axis=dim)


def regroup_near(x):
    size = lax.axis_size("docs")
    core = lax.axis_index("docs") % CORES
    half = x.shape[1] // CORES
    kept = lax.dynamic_slice_in_dim(x, core * half, half, 1)
    given = lax.dynamic_slice_in_dim(x, (1 - core) * half, half, 1)
    return jnp.concatenate(in_order([kept, xor_permute(given, "docs", size, 1)], core), axis=0)


def regroup_far(x):
    size = lax.axis_size("docs")
    places = size // CORES
    place = lax.axis_index("docs") // CORES
    chunk = x.shape[1] // places
    parts = [lax.dynamic_slice_in_dim(x, place * chunk, chunk, 1)]
    for s in range(1, places):
        piece = lax.dynamic_slice_in_dim(x, (place ^ s) * chunk, chunk, 1)
        parts.append(xor_permute(piece, "docs", size, CORES * s))
    return parts


def own_tokens(x):
    size = lax.axis_size("docs")
    me = lax.axis_index("docs")
    core, place = me % CORES, me // CORES
    places = size // CORES
    x = x.reshape(places, CORES, x.shape[0] // size, x.shape[1])
    kept = lax.dynamic_index_in_dim(x, core, 1, keepdims=False)
    given = lax.dynamic_index_in_dim(x, 1 - core, 1, keepdims=False)
    chip = kept + xor_permute(given, "docs", size, 1)
    return scatter_direct(chip, "docs", places, place, CORES, 0, f32)[0]


def spread_left(block):
    size = lax.axis_size("docs")
    places = size // CORES
    me = lax.axis_index("docs") // CORES
    here = lax.axis_index("basis")
    left = jnp.where(me == here, block, jnp.zeros_like(block))
    for s in range(1, places):
        pairs = [
            (b * size + b * CORES + c, b * size + (b ^ s) * CORES + c)
            for b in range(places)
            for c in range(CORES)
        ]
        left = left + lax.ppermute(block, ("basis", "docs"), pairs)
    return left


def join_cores(x):
    size = lax.axis_size("docs")
    core = lax.axis_index("docs") % CORES
    return jnp.concatenate(in_order([x, xor_permute(x, "docs", size, 1)], core), axis=1)


def moment_kernel(width, out_ref, in_ref, values_ref, test_ref, *refs):
    moment_refs, sketch_ref = refs[:QUERIES], refs[QUERIES]
    rows, cols = values_ref.shape
    sides = [out_ref[:, q * LQ : (q + 1) * LQ] for q in range(QUERIES)]

    def step(c, carry):
        at = pl.ds(pl.multiple_of(c * width, width), width)
        weight = 1.0 / (values_ref[:, at].astype(f32) + damping)
        for q in range(QUERIES):
            product = jnp.dot(
                sides[q], in_ref[q * LQ : (q + 1) * LQ, at], preferred_element_type=f32
            )
            moment_refs[q][:, at] = (product * weight).astype(bf16)
        return carry

    lax.fori_loop(0, cols // width, step, 0)
    for q in range(QUERIES):
        sketch_ref[q * RANK : (q + 1) * RANK, :] = lax.dot_general(
            test_ref[...],
            moment_refs[q][...],
            (((1,), (1,)), ((), ())),
            preferred_element_type=f32,
        )


def moment_pass(rot_out, rot_in, eigvals, test):
    rows, cols = eigvals.shape
    height = tile(rows, 256, 128)
    width = tile(cols, 1792, 128)
    *moments, sketch = pl.pallas_call(
        functools.partial(moment_kernel, width),
        out_shape=[jax.ShapeDtypeStruct((rows, cols), bf16)] * QUERIES
        + [jax.ShapeDtypeStruct((QUERIES * RANK, rows), f32)],
        grid=(rows // height,),
        in_specs=[
            pl.BlockSpec((height, rot_out.shape[1]), lambda i: (i, 0)),
            pl.BlockSpec(rot_in.shape, lambda i: (0, 0)),
            pl.BlockSpec((height, cols), lambda i: (i, 0)),
            pl.BlockSpec(test.shape, lambda i: (0, 0)),
        ],
        out_specs=[pl.BlockSpec((height, cols), lambda i: (i, 0))] * QUERIES
        + [pl.BlockSpec((QUERIES * RANK, height), lambda i: (0, i))],
        compiler_params=params(),
        cost_estimate=pl.CostEstimate(
            flops=4 * 2 * QUERIES * rows * cols * 256,
            bytes_accessed=QUERIES * rows * cols * 2 + rows * cols * 2,
            transcendentals=0,
        ),
        name="moment_pass",
    )(rot_out, rot_in, eigvals, test)
    return moments, sketch


def cross_kernel(sketch_ref, *refs):
    cross_ref = refs[QUERIES]
    for q in range(QUERIES):
        cross_ref[q * RANK : (q + 1) * RANK, :] = jnp.dot(
            sketch_ref[q * RANK : (q + 1) * RANK, :], refs[q][...], preferred_element_type=f32
        )


def cross_pass(sketch, moments):
    rows, cols = moments[0].shape
    width = tile(cols, 512, 128)
    return pl.pallas_call(
        cross_kernel,
        out_shape=jax.ShapeDtypeStruct((QUERIES * RANK, cols), f32),
        grid=(cols // width,),
        in_specs=[pl.BlockSpec(sketch.shape, lambda j: (0, 0))]
        + [pl.BlockSpec((rows, width), lambda j: (0, j))] * QUERIES,
        out_specs=pl.BlockSpec((QUERIES * RANK, width), lambda j: (0, j)),
        compiler_params=params(),
        cost_estimate=pl.CostEstimate(
            flops=2 * QUERIES * rows * cols * 256,
            bytes_accessed=QUERIES * rows * cols * 2,
            transcendentals=0,
        ),
        name="cross_pass",
    )(sketch, *moments)


def inverse_kernel(gram_ref, out_ref):
    gram = gram_ref[...]
    row = lax.broadcasted_iota(jnp.int32, gram.shape, 1)
    col = lax.broadcasted_iota(jnp.int32, gram.shape, 2)
    unit = jnp.where(row == col, 1.0, 0.0).astype(f32)
    below = lax.broadcasted_iota(jnp.int32, (gram.shape[0], RANK, 1), 1)
    for k in range(RANK):
        pivot = gram[:, k : k + 1, k : k + 1]
        factor = jnp.where(below > k, gram[:, :, k : k + 1] / pivot, 0.0)
        unit = unit - factor * unit[:, k : k + 1, :]
        gram = gram - factor * gram[:, k : k + 1, :]
    diagonal = jnp.sum(jnp.where(row == col, gram, 0.0), axis=2, keepdims=True)
    out_ref[...] = unit / jnp.sqrt(diagonal)


def inverse_factor(gram):
    return pl.pallas_call(
        inverse_kernel,
        out_shape=jax.ShapeDtypeStruct(gram.shape, f32),
        compiler_params=params(),
        name="inverse_factor",
    )(gram)


def right_kernel(parts, *refs):
    projected_ref, out_ref, across_ref = refs[parts:]

    @pl.when(pl.program_id(0) == 0)
    def _():
        across_ref[...] = jnp.transpose(projected_ref[...].astype(f32)).astype(bf16)

    height = refs[0].shape[0]
    for n in range(parts):
        out_ref[n * height : (n + 1) * height, :] = jnp.dot(
            refs[n][...], across_ref[...], preferred_element_type=f32
        ).astype(out_ref.dtype)


def right_pass(eig_in, projected):
    rows, cols = eig_in.shape
    parts = 4
    height = tile(rows // parts, 256, 16)
    width = projected.shape[0]
    return pl.pallas_call(
        functools.partial(right_kernel, parts),
        out_shape=jax.ShapeDtypeStruct((rows, width), bf16),
        grid=(rows // (parts * height),),
        in_specs=[
            pl.BlockSpec((height, cols), lambda i, n=n: (parts * i + n, 0)) for n in range(parts)
        ]
        + [pl.BlockSpec(projected.shape, lambda i: (0, 0))],
        out_specs=pl.BlockSpec((parts * height, width), lambda i: (i, 0)),
        scratch_shapes=[pltpu.VMEM(projected.shape[::-1], bf16)],
        compiler_params=params(),
        cost_estimate=pl.CostEstimate(
            flops=2 * rows * cols * 256,
            bytes_accessed=rows * cols * 2,
            transcendentals=0,
        ),
        name="right_pass",
    )(*[eig_in] * parts, projected)


def rotate_in(eig_in, in_factors):
    size = lax.axis_size("docs")
    places = size // CORES
    me = lax.axis_index("docs")
    core, place = me % CORES, me // CORES
    chunks = [in_factors]
    depth = CORES * in_factors.shape[0]
    totals = []
    for s in range(places):
        low = s & -s
        if s == low and s > 0:
            chunks.append(xor_permute(in_factors, "docs", size, CORES * s))
        elif s > 0:
            chunks.append(xor_permute(chunks[s - low], "docs", size, CORES * low))
        chunk = chunks[s]
        if s > 1:
            chunk = chunks[s] = hold(chunk, totals[0 if s == low else 1])
        mate = xor_permute(chunk, "docs", size, 1)
        both = jnp.concatenate(in_order([chunk, mate], core), axis=0)
        rows = lax.dynamic_slice_in_dim(eig_in, (place ^ s) * depth, depth, 0)
        product = lax.dot_general(
            both, rows, (((0,), (0,)), ((), ())), preferred_element_type=f32
        )
        totals.append(totals[-1] + product if totals else product)
    return totals[-1]


def local(
    eig_in,
    eig_out,
    eigvals,
    out_factors,
    in_factors,
    test_matrix,
    activations,
    gradients,
    doc_lengths,
):
    cols_in = eig_in.shape[1]
    tok_count = activations.shape[0]
    basis = lax.axis_size("basis")
    docs = lax.axis_size("docs")

    part_out = jnp.dot(eig_out, out_factors, preferred_element_type=f32)
    part_in = rotate_in(eig_in, in_factors)
    rot_in, (early, late) = reduce_rotated(part_in)
    rot_out = scatter_docs(part_out, 0, f32, bf16, after=part_in)
    rot_out = gather_docs(hold(rot_out, *early), 0)

    moments, part = moment_pass(rot_out, rot_in, eigvals, jnp.transpose(test_matrix))
    all_tokens = regroup_far(hold(regroup_near(activations), late[1]))
    part = hold(part, *all_tokens[1:])
    sketch = gather_docs(scatter_docs(part, 1, f32, bf16), 1)
    split = sketch.reshape(QUERIES, RANK, sketch.shape[1])
    gram = jnp.einsum("qri,qsi->qrs", split, split, preferred_element_type=f32)
    gram = tree_sum([gram] + [xor_permute(gram, "basis", basis, s) for s in range(1, basis)])
    cross = cross_pass(sketch, moments)
    back = jnp.dot(sketch, eig_out, preferred_element_type=f32)
    inverse = inverse_factor(gram)
    both = jnp.concatenate([cross, back], axis=1)
    solved = jnp.einsum(
        "qkr,qrj->qkj",
        inverse,
        both.reshape(QUERIES, RANK, both.shape[1]),
        precision=highest,
        preferred_element_type=f32,
    ).reshape(both.shape)
    solved = reduce_basis(solved, 0)
    projected = solved[:, :cols_in]
    left = spread_left(solved[:, cols_in:])
    right = hold(right_pass(eig_in, projected), left)
    token_out = lax.dot_general(
        gradients, join_cores(left), (((1,), (1,)), ((), ())), preferred_element_type=f32
    )
    right = scatter_docs(right, 0, bf16, bf16)
    all_tokens = jnp.concatenate(in_order(all_tokens, lax.axis_index("docs") // CORES), axis=0)
    token_in = own_tokens(jnp.dot(all_tokens, right, preferred_element_type=f32))

    tokens = jnp.concatenate([token_in, token_out], axis=1)
    tokens = tree_sum(
        [tokens] + [xor_permute(tokens, "basis", basis, s) for s in range(1, basis)]
    )
    width = QUERIES * RANK
    scores = (tokens[:, :width] * tokens[:, width:]).reshape(tok_count, QUERIES, RANK).sum(axis=2)
    positions = lax.axis_index("docs") * tok_count + jnp.arange(tok_count, dtype=jnp.int32)
    doc_ends = jnp.cumsum(doc_lengths)
    doc_starts = doc_ends - doc_lengths
    member = (
        (positions[:, None] >= doc_starts[None, :]) & (positions[:, None] < doc_ends[None, :])
    ).astype(f32)
    doc_part = lax.dot_general(member, scores, (((0,), (0,)), ((), ())), precision=highest)
    doc_part = doc_part + xor_permute(doc_part, "docs", docs, 1)
    doc_influence = tree_sum(
        [doc_part]
        + [xor_permute(doc_part, "docs", docs, CORES * s) for s in range(1, docs // CORES)]
    )
    return (scores, doc_influence)


def solution(mesh):
    return jax.shard_map(
        local,
        mesh=mesh,
        in_specs=(
            P("basis", "docs"),
            P("basis", "docs"),
            P("basis", "docs"),
            P("docs", None),
            P(("basis", "docs"), None),
            P("docs", None),
            P("docs", "basis"),
            P("docs", "basis"),
            P(),
        ),
        out_specs=(P("docs", None), P()),
        check_vma=False,
    )
```

```python
import functools

import jax
import jax.numpy as jnp
import numpy as np
from jax import lax
from jax.experimental import pallas as pl
from jax.experimental.pallas import tpu as pltpu
from jax.sharding import PartitionSpec as P

QUERIES = 4
LQ = 64
RANK = 32
CORES = 2
VMEM = 56 * 1024 * 1024

damping = 0.1
highest = lax.Precision.HIGHEST
f32 = jnp.float32
bf16 = jnp.bfloat16


def tile(extent, most, unit):
    best = extent
    for size in range(unit, min(most, extent) + 1, unit):
        if extent % size == 0:
            best = size
    return best


def params():
    return pltpu.CompilerParams(vmem_limit_bytes=VMEM)


def hold(x, *others):
    other = sum(other[:16, :128].astype(f32) for other in others)
    return pl.pallas_call(
        lambda *refs: None,
        out_shape=jax.ShapeDtypeStruct(x.shape, x.dtype),
        in_specs=[pl.BlockSpec(memory_space=pl.ANY)] * 2,
        out_specs=pl.BlockSpec(memory_space=pl.ANY),
        input_output_aliases={0: 0},
        name="hold",
    )(x, other)


def xor_permute(x, axis, size, bits):
    return lax.ppermute(x, axis, [(i, i ^ bits) for i in range(size)])


def tree_sum(parts):
    while len(parts) > 1:
        parts = [parts[i] + parts[i + 1] for i in range(0, len(parts), 2)]
    return parts[0]


def in_order(parts, me):
    bit = 1
    while bit < len(parts):
        on = (me & bit) != 0
        parts = [jnp.where(on, parts[s ^ bit], parts[s]) for s in range(len(parts))]
        bit *= 2
    return parts


def scatter_direct(x, axis, size, me, unit, dim, kind):
    chunk = x.shape[dim] // size
    total = lax.dynamic_slice_in_dim(x, me * chunk, chunk, dim).astype(f32)
    low = x.astype(kind)
    whole = lax.axis_size(axis)
    for s in range(1, size):
        piece = lax.dynamic_slice_in_dim(low, (me ^ s) * chunk, chunk, dim)
        total = total + xor_permute(piece, axis, whole, unit * s).astype(f32)
    return total


def gather_direct(y, axis, size, me, unit, dim):
    whole = lax.axis_size(axis)
    parts = [y] + [xor_permute(y, axis, whole, unit * s) for s in range(1, size)]
    return jnp.concatenate(in_order(parts, me), axis=dim)


def reduce_basis(x, dim):
    size = lax.axis_size("basis")
    me = lax.axis_index("basis")
    mine = scatter_direct(x, "basis", size, me, 1, dim, bf16).astype(bf16)
    return gather_direct(mine, "basis", size, me, 1, dim)


def halve_basis(x, bits):
    size = lax.axis_size("basis")
    me = lax.axis_index("basis")
    for n, bit in enumerate(bits):
        half = x.shape[0] // 2
        on = (me & bit) // bit
        kept = lax.dynamic_slice_in_dim(x, on * half, half, 0)
        given = lax.dynamic_slice_in_dim(x, (1 - on) * half, half, 0)
        x = kept + xor_permute(given.astype(f32 if n else bf16), "basis", size, bit).astype(f32)
        if n == 0:
            early = x
    x = x.astype(bf16)
    for bit in bits[::-1]:
        on = (me & bit) // bit
        late = x
        x = jnp.concatenate(in_order([x, xor_permute(x, "basis", size, bit)], on), axis=0)
    return x, early, late


def reduce_rotated(x):
    bits = []
    while 1 << len(bits) < lax.axis_size("basis"):
        bits.append(1 << len(bits))
    half = x.shape[0] // 2
    upper, *upper_marks = halve_basis(x[:half], bits)
    lower, *lower_marks = halve_basis(x[half:], bits[::-1])
    return jnp.concatenate([upper, lower], axis=0), list(zip(upper_marks, lower_marks))


def scatter_docs(x, dim, near, far, after=None):
    size = lax.axis_size("docs")
    me = lax.axis_index("docs")
    core, place = me % CORES, me // CORES
    half = x.shape[dim] // CORES
    kept = lax.dynamic_slice_in_dim(x, core * half, half, dim).astype(f32)
    given = lax.dynamic_slice_in_dim(x, (1 - core) * half, half, dim).astype(near)
    chip = kept + xor_permute(given, "docs", size, 1).astype(f32)
    if after is not None:
        chip = hold(chip, after)
    return scatter_direct(chip, "docs", size // CORES, place, CORES, dim, far).astype(bf16)


def gather_docs(mine, dim):
    size = lax.axis_size("docs")
    me = lax.axis_index("docs")
    core, place = me % CORES, me // CORES
    ours = gather_direct(mine, "docs", size // CORES, place, CORES, dim)
    theirs = xor_permute(ours, "docs", size, 1)
    return jnp.concatenate(in_order([ours, theirs], core), axis=dim)


def regroup_near(x):
    size = lax.axis_size("docs")
    core = lax.axis_index("docs") % CORES
    half = x.shape[1] // CORES
    kept = lax.dynamic_slice_in_dim(x, core * half, half, 1)
    given = lax.dynamic_slice_in_dim(x, (1 - core) * half, half, 1)
    return jnp.concatenate(in_order([kept, xor_permute(given, "docs", size, 1)], core), axis=0)


def regroup_far(x):
    size = lax.axis_size("docs")
    places = size // CORES
    place = lax.axis_index("docs") // CORES
    chunk = x.shape[1] // places
    parts = [lax.dynamic_slice_in_dim(x, place * chunk, chunk, 1)]
    for s in range(1, places):
        piece = lax.dynamic_slice_in_dim(x, (place ^ s) * chunk, chunk, 1)
        parts.append(xor_permute(piece, "docs", size, CORES * s))
    return parts


def own_tokens(x):
    size = lax.axis_size("docs")
    me = lax.axis_index("docs")
    core, place = me % CORES, me // CORES
    places = size // CORES
    x = x.reshape(places, CORES, x.shape[0] // size, x.shape[1])
    kept = lax.dynamic_index_in_dim(x, core, 1, keepdims=False)
    given = lax.dynamic_index_in_dim(x, 1 - core, 1, keepdims=False)
    chip = kept + xor_permute(given, "docs", size, 1)
    return scatter_direct(chip, "docs", places, place, CORES, 0, f32)[0]


def spread_left(block):
    size = lax.axis_size("docs")
    places = size // CORES
    me = lax.axis_index("docs") // CORES
    here = lax.axis_index("basis")
    left = jnp.where(me == here, block, jnp.zeros_like(block))
    for s in range(1, places):
        pairs = [
            (b * size + b * CORES + c, b * size + (b ^ s) * CORES + c)
            for b in range(places)
            for c in range(CORES)
        ]
        left = left + lax.ppermute(block, ("basis", "docs"), pairs)
    return left


def join_cores(x):
    size = lax.axis_size("docs")
    core = lax.axis_index("docs") % CORES
    return jnp.concatenate(in_order([x, xor_permute(x, "docs", size, 1)], core), axis=1)


def moment_kernel(width, out_ref, in_ref, values_ref, test_ref, *refs):
    moment_refs, sketch_ref = refs[:QUERIES], refs[QUERIES]
    rows, cols = values_ref.shape
    sides = [out_ref[:, q * LQ : (q + 1) * LQ] for q in range(QUERIES)]

    def step(c, carry):
        at = pl.ds(pl.multiple_of(c * width, width), width)
        weight = 1.0 / (values_ref[:, at].astype(f32) + damping)
        for q in range(QUERIES):
            product = jnp.dot(
                sides[q], in_ref[q * LQ : (q + 1) * LQ, at], preferred_element_type=f32
            )
            moment_refs[q][:, at] = (product * weight).astype(bf16)
        return carry

    lax.fori_loop(0, cols // width, step, 0)
    for q in range(QUERIES):
        sketch_ref[q * RANK : (q + 1) * RANK, :] = lax.dot_general(
            test_ref[...],
            moment_refs[q][...],
            (((1,), (1,)), ((), ())),
            preferred_element_type=f32,
        )


def moment_pass(rot_out, rot_in, eigvals, test):
    rows, cols = eigvals.shape
    height = tile(rows, 256, 128)
    width = tile(cols, 1792, 128)
    *moments, sketch = pl.pallas_call(
        functools.partial(moment_kernel, width),
        out_shape=[jax.ShapeDtypeStruct((rows, cols), bf16)] * QUERIES
        + [jax.ShapeDtypeStruct((QUERIES * RANK, rows), f32)],
        grid=(rows // height,),
        in_specs=[
            pl.BlockSpec((height, rot_out.shape[1]), lambda i: (i, 0)),
            pl.BlockSpec(rot_in.shape, lambda i: (0, 0)),
            pl.BlockSpec((height, cols), lambda i: (i, 0)),
            pl.BlockSpec(test.shape, lambda i: (0, 0)),
        ],
        out_specs=[pl.BlockSpec((height, cols), lambda i: (i, 0))] * QUERIES
        + [pl.BlockSpec((QUERIES * RANK, height), lambda i: (0, i))],
        compiler_params=params(),
        cost_estimate=pl.CostEstimate(
            flops=4 * 2 * QUERIES * rows * cols * 256,
            bytes_accessed=QUERIES * rows * cols * 2 + rows * cols * 2,
            transcendentals=0,
        ),
        name="moment_pass",
    )(rot_out, rot_in, eigvals, test)
    return moments, sketch


def cross_kernel(sketch_ref, *refs):
    cross_ref = refs[QUERIES]
    for q in range(QUERIES):
        cross_ref[q * RANK : (q + 1) * RANK, :] = jnp.dot(
            sketch_ref[q * RANK : (q + 1) * RANK, :], refs[q][...], preferred_element_type=f32
        )


def cross_pass(sketch, moments):
    rows, cols = moments[0].shape
    width = tile(cols, 512, 128)
    return pl.pallas_call(
        cross_kernel,
        out_shape=jax.ShapeDtypeStruct((QUERIES * RANK, cols), f32),
        grid=(cols // width,),
        in_specs=[pl.BlockSpec(sketch.shape, lambda j: (0, 0))]
        + [pl.BlockSpec((rows, width), lambda j: (0, j))] * QUERIES,
        out_specs=pl.BlockSpec((QUERIES * RANK, width), lambda j: (0, j)),
        compiler_params=params(),
        cost_estimate=pl.CostEstimate(
            flops=2 * QUERIES * rows * cols * 256,
            bytes_accessed=QUERIES * rows * cols * 2,
            transcendentals=0,
        ),
        name="cross_pass",
    )(sketch, *moments)


def inverse_kernel(gram_ref, out_ref):
    gram = gram_ref[...]
    row = lax.broadcasted_iota(jnp.int32, gram.shape, 1)
    col = lax.broadcasted_iota(jnp.int32, gram.shape, 2)
    unit = jnp.where(row == col, 1.0, 0.0).astype(f32)
    below = lax.broadcasted_iota(jnp.int32, (gram.shape[0], RANK, 1), 1)
    for k in range(RANK):
        pivot = gram[:, k : k + 1, k : k + 1]
        factor = jnp.where(below > k, gram[:, :, k : k + 1] / pivot, 0.0)
        unit = unit - factor * unit[:, k : k + 1, :]
        gram = gram - factor * gram[:, k : k + 1, :]
    diagonal = jnp.sum(jnp.where(row == col, gram, 0.0), axis=2, keepdims=True)
    out_ref[...] = unit / jnp.sqrt(diagonal)


def inverse_factor(gram):
    return pl.pallas_call(
        inverse_kernel,
        out_shape=jax.ShapeDtypeStruct(gram.shape, f32),
        compiler_params=params(),
        name="inverse_factor",
    )(gram)


def right_kernel(parts, *refs):
    projected_ref, out_ref, across_ref = refs[parts:]

    @pl.when(pl.program_id(0) == 0)
    def _():
        across_ref[...] = jnp.transpose(projected_ref[...].astype(f32)).astype(bf16)

    height = refs[0].shape[0]
    for n in range(parts):
        out_ref[n * height : (n + 1) * height, :] = jnp.dot(
            refs[n][...], across_ref[...], preferred_element_type=f32
        ).astype(out_ref.dtype)


def right_pass(eig_in, projected):
    rows, cols = eig_in.shape
    parts = 4
    height = tile(rows // parts, 256, 16)
    width = projected.shape[0]
    return pl.pallas_call(
        functools.partial(right_kernel, parts),
        out_shape=jax.ShapeDtypeStruct((rows, width), bf16),
        grid=(rows // (parts * height),),
        in_specs=[
            pl.BlockSpec((height, cols), lambda i, n=n: (parts * i + n, 0)) for n in range(parts)
        ]
        + [pl.BlockSpec(projected.shape, lambda i: (0, 0))],
        out_specs=pl.BlockSpec((parts * height, width), lambda i: (i, 0)),
        scratch_shapes=[pltpu.VMEM(projected.shape[::-1], bf16)],
        compiler_params=params(),
        cost_estimate=pl.CostEstimate(
            flops=2 * rows * cols * 256,
            bytes_accessed=rows * cols * 2,
            transcendentals=0,
        ),
        name="right_pass",
    )(*[eig_in] * parts, projected)


def rotate_in(eig_in, in_factors):
    size = lax.axis_size("docs")
    places = size // CORES
    me = lax.axis_index("docs")
    core, place = me % CORES, me // CORES
    chunks = [in_factors]
    depth = CORES * in_factors.shape[0]
    totals = []
    for s in range(places):
        low = s & -s
        if s == low and s > 0:
            chunks.append(xor_permute(in_factors, "docs", size, CORES * s))
        elif s > 0:
            chunks.append(xor_permute(chunks[s - low], "docs", size, CORES * low))
        chunk = chunks[s]
        if s != low:
            chunk = chunks[s] = hold(chunk, totals[1])
        mate = xor_permute(chunk, "docs", size, 1)
        both = jnp.concatenate(in_order([chunk, mate], core), axis=0)
        rows = lax.dynamic_slice_in_dim(eig_in, (place ^ s) * depth, depth, 0)
        product = lax.dot_general(
            both, rows, (((0,), (0,)), ((), ())), preferred_element_type=f32
        )
        totals.append(totals[-1] + product if totals else product)
    return totals[-1]


def local(
    eig_in,
    eig_out,
    eigvals,
    out_factors,
    in_factors,
    test_matrix,
    activations,
    gradients,
    doc_lengths,
):
    cols_in = eig_in.shape[1]
    tok_count = activations.shape[0]
    basis = lax.axis_size("basis")
    docs = lax.axis_size("docs")

    part_out = jnp.dot(eig_out, out_factors, preferred_element_type=f32)
    part_in = rotate_in(eig_in, in_factors)
    rot_in, (early, late) = reduce_rotated(part_in)
    rot_out = scatter_docs(part_out, 0, f32, bf16, after=part_in)
    rot_out = gather_docs(hold(rot_out, *early), 0)

    moments, part = moment_pass(rot_out, rot_in, eigvals, jnp.transpose(test_matrix))
    all_tokens = regroup_far(hold(regroup_near(activations), late[1]))
    part = hold(part, *all_tokens[1:])
    sketch = gather_docs(scatter_docs(part, 1, f32, bf16), 1)
    split = sketch.reshape(QUERIES, RANK, sketch.shape[1])
    gram = jnp.einsum("qri,qsi->qrs", split, split, preferred_element_type=f32)
    gram = tree_sum([gram] + [xor_permute(gram, "basis", basis, s) for s in range(1, basis)])
    cross = cross_pass(sketch, moments)
    back = jnp.dot(sketch, eig_out, preferred_element_type=f32)
    inverse = inverse_factor(gram)
    both = jnp.concatenate([cross, back], axis=1)
    solved = jnp.einsum(
        "qkr,qrj->qkj",
        inverse,
        both.reshape(QUERIES, RANK, both.shape[1]),
        precision=highest,
        preferred_element_type=f32,
    ).reshape(both.shape)
    solved = reduce_basis(solved, 0)
    projected = solved[:, :cols_in]
    left = spread_left(solved[:, cols_in:])
    right = hold(right_pass(eig_in, projected), left)
    token_out = lax.dot_general(
        gradients, join_cores(left), (((1,), (1,)), ((), ())), preferred_element_type=f32
    )
    right = scatter_docs(right, 0, bf16, bf16)
    all_tokens = jnp.concatenate(in_order(all_tokens, lax.axis_index("docs") // CORES), axis=0)
    token_in = own_tokens(jnp.dot(all_tokens, right, preferred_element_type=f32))

    tokens = jnp.concatenate([token_in, token_out], axis=1)
    tokens = tree_sum(
        [tokens] + [xor_permute(tokens, "basis", basis, s) for s in range(1, basis)]
    )
    width = QUERIES * RANK
    scores = (tokens[:, :width] * tokens[:, width:]).reshape(tok_count, QUERIES, RANK).sum(axis=2)
    positions = lax.axis_index("docs") * tok_count + jnp.arange(tok_count, dtype=jnp.int32)
    doc_ends = jnp.cumsum(doc_lengths)
    doc_starts = doc_ends - doc_lengths
    member = (
        (positions[:, None] >= doc_starts[None, :]) & (positions[:, None] < doc_ends[None, :])
    ).astype(f32)
    doc_part = lax.dot_general(member, scores, (((0,), (0,)), ((), ())), precision=highest)
    doc_part = doc_part + xor_permute(doc_part, "docs", docs, 1)
    doc_influence = tree_sum(
        [doc_part]
        + [xor_permute(doc_part, "docs", docs, CORES * s) for s in range(1, docs // CORES)]
    )
    return (scores, doc_influence)


def solution(mesh):
    return jax.shard_map(
        local,
        mesh=mesh,
        in_specs=(
            P("basis", "docs"),
            P("basis", "docs"),
            P("basis", "docs"),
            P("docs", None),
            P(("basis", "docs"), None),
            P("docs", None),
            P("docs", "basis"),
            P("docs", "basis"),
            P(),
        ),
        out_specs=(P("docs", None), P()),
        check_vma=False,
    )
```
